512 devices in a mesh: dp: 64 (over z, y), tensor: 8 (over x, core).
Axes of the slice: x: 4, y: 8, z: 8, core: 2. Of those that a mesh axis runs over, the one named last changes fastest.
Arguments:
- activations: bfloat16 [16384, 4096], P(('dp', 'tensor')), may hold values from -24 to 24
- cotangent: bfloat16 [16384, 4096], P(('dp', 'tensor')), may hold values from -24 to 24
- gate_pre: bfloat16 [16384, 16384], P('dp', 'tensor'), may hold values from -8 to 8
- up_value: bfloat16 [16384, 16384], P('dp', 'tensor'), may hold values from -6 to 6
- hidden_grad: bfloat16 [16384, 16384], P('dp', 'tensor'), may hold values from -16 to 16
- warm_factors: float32 [2, 8, 4096, 128], P(None, 'tensor', 'dp'), may hold values from -6 to 6
Outputs:
- left_united: float32 [8, 4096, 128], P('tensor', 'dp')
- left_down: float32 [8, 2048, 128], P('tensor', 'dp')
- right_factors: float32 [2, 8, 4096, 128], P(None, 'tensor', 'dp')
The draws below stay inside these ranges and needn't reach their ends.
All inputs are finite; a program needn't handle non-finite values.
Results may differ from the reference program's by a relative error of at most 0.0031.
Values may be sent and summed in bfloat16 or wider, within the bound.
A program may use at most 64 MiB of HBM per device.

```python
import jax
import jax.numpy as jnp
from jax import lax

D = 4096
FF_DEV = 2048
RANK = 128
FF = 16384
TOKENS = 16384
N_DP = 64
N_TENSOR = 8


def strengthened(values, rng, source, target, blocks, factor):
    owner, partner = [(jnp.arange(values.shape[dim]) // (values.shape[dim] // blocks)).reshape([-1 if axis == dim else 1 for axis in range(values.ndim)]) for dim in (source, target)]
    chosen = jax.random.permutation(rng, blocks)[partner]
    strong = (owner == chosen) | (owner == (partner + blocks // 2) % blocks)
    return jnp.where(strong, factor * values, values)


def shard_levels(stream_key, dims, shards, low, high):
    level, own = 1.0, jax.random.fold_in(stream_key, 6)
    for axis_at, blocks in shards:
        draws = jnp.exp(jax.random.uniform(jax.random.fold_in(own, axis_at), (blocks,), jnp.float32, low / len(shards), high / len(shards)))
        level = level * jnp.repeat(draws, dims[axis_at] // blocks).reshape([-1 if axis == axis_at else 1 for axis in range(len(dims))])
    return level


def centred(key, dims, deviation, most, cuts=(), kind=jnp.bfloat16):
    level = shard_levels(key, dims, cuts, -0.22, 0.18) if cuts else 1.0
    values = jax.random.normal(key, dims, jnp.float32) * deviation * level
    return jnp.minimum(jnp.maximum(values, -most), most).astype(kind)


def gaussian_with(own_key, dims, scale, bound, shards, heavy, kind=jnp.bfloat16):
    values = scale * jax.random.normal(own_key, dims, jnp.float32)
    if shards:
        values = values * shard_levels(own_key, dims, shards, -0.22, 0.18)
    return jnp.clip(strengthened(values, jax.random.fold_in(own_key, 3), *heavy), -bound, bound).astype(kind)


def setup_inputs(seed: int = 0) -> dict:
    key_of = jax.random.split(jax.random.key(seed), 7)
    return {
        "activations": gaussian_with(key_of[0], (TOKENS, D), 1.0, 24.0, ((0, 512),), (0, 1, 512, 6.0)),
        "cotangent": gaussian_with(key_of[1], (TOKENS, D), 1.0, 24.0, ((0, 512),), (0, 1, 512, 6.0)),
        "gate_pre": centred(key_of[2], (TOKENS, FF), 2.0, 8.0, ((0, 64), (1, 8))),
        "up_value": centred(key_of[3], (TOKENS, FF), 1.0, 6.0, ((0, 64), (1, 8))),
        "hidden_grad": gaussian_with(key_of[4], (TOKENS, FF), 1.0, 16.0, ((0, 64), (1, 8)), (0, 1, 64, 4.0)),
        "warm_factors": centred(key_of[5], (2, N_TENSOR, D, RANK), 1.0, 6.0, ((1, 8), (2, 64)), jnp.float32),
    }


def orthonormal(matrix):
    count = matrix.shape[1]

    def settle(position, settled):
        place = jnp.asarray(position).astype(jnp.int32)
        vector = lax.dynamic_slice_in_dim(matrix, place, 1, 1)
        coeffs = jnp.dot(settled.T, vector, precision=lax.Precision.HIGHEST)
        vector = vector - jnp.dot(settled, coeffs, precision=lax.Precision.HIGHEST)
        vector = vector / jnp.sqrt(jnp.sum(vector * vector))
        return lax.dynamic_update_slice_in_dim(settled, vector, place, 1)
    return lax.fori_loop(0, count, settle, jnp.zeros_like(matrix))

def reference(activations, cotangent, gate_pre, up_value, hidden_grad, warm_factors):
    acts_wide = activations.astype(jnp.float32)
    cotan_wide = cotangent.astype(jnp.float32)

    def split_blocks(array):
        return jnp.transpose(array.reshape(TOKENS, N_TENSOR, FF_DEV), (1, 0, 2))

    def block_pass(pieces):
        gate_block, up_block, hgrad_block, warm_block = pieces
        gate_wide = gate_block.astype(jnp.float32)
        up_wide = up_block.astype(jnp.float32)
        hgrad_wide = hgrad_block.astype(jnp.float32)
        sigma = jax.nn.sigmoid(gate_wide)
        active = gate_wide * sigma
        hidden = (active * up_wide).astype(jnp.bfloat16)
        gate_back = (hgrad_wide * up_wide * sigma * (1.0 + gate_wide * (1.0 - sigma))).astype(jnp.bfloat16)
        up_back = (hgrad_wide * active).astype(jnp.bfloat16)
        united = jnp.concatenate([gate_back, up_back], axis=1).astype(jnp.float32)
        hidden_wide = hidden.astype(jnp.float32)
        probe_united = jnp.dot(acts_wide, warm_block[0], precision=lax.Precision.HIGHEST)
        probe_down = jnp.dot(cotan_wide, warm_block[1], precision=lax.Precision.HIGHEST)
        left_one = orthonormal(jnp.dot(united.T, probe_united, precision=lax.Precision.HIGHEST))
        left_two = orthonormal(jnp.dot(hidden_wide.T, probe_down, precision=lax.Precision.HIGHEST))
        mixed_one = jnp.dot(united, left_one, precision=lax.Precision.HIGHEST)
        mixed_two = jnp.dot(hidden_wide, left_two, precision=lax.Precision.HIGHEST)
        right_one = jnp.dot(acts_wide.T, mixed_one, precision=lax.Precision.HIGHEST) / N_DP
        right_two = jnp.dot(cotan_wide.T, mixed_two, precision=lax.Precision.HIGHEST) / N_DP
        return (left_one, left_two, jnp.stack([right_one, right_two]))
    left_united, left_down, right = lax.map(block_pass, (split_blocks(gate_pre), split_blocks(up_value), split_blocks(hidden_grad), jnp.transpose(warm_factors, (1, 0, 2, 3))))
    return (left_united, left_down, jnp.transpose(right, (1, 0, 2, 3)))
```

```python
import functools

import jax
import jax.numpy as jnp
from jax import lax
from jax.experimental import pallas as pl
from jax.experimental.pallas import tpu as pltpu
from jax.sharding import PartitionSpec as P

F32 = jnp.float32
BF16 = jnp.bfloat16
RANK = 128
CUT = 48
PANEL = 16


def tdot(left, right):
    return lax.dot_general(left, right, (((0,), (0,)), ((), ())), preferred_element_type=F32)


def two_halves(values):
    high = values.astype(BF16)
    low = (values - high.astype(F32)).astype(BF16)
    return jnp.concatenate([high, low], axis=1)


def kernel(nz, ny, nt, acts_in, cot_in, gate_in, up_in, hg_in, warm_in,
           left_u_out, left_d_out, right_out,
           acts, cot, gate, up, hg, warm,
           gate_back, up_back, hidden,
           part_a, part_b, got_a, got_b, sum_a, sum_b, fin_a, fin_b,
           raw_u, raw_d, all_u, all_d,
           rpart_a, rpart_b, rgot_a, rgot_b, rsum_a, rsum_b, rfin_a, rfin_b,
           gram,
           load_sem, tok_send, tok_recv, first_send, first_recv,
           ring_send, ring_recv, one_send, one_recv, two_send, two_recv):
    d = lax.axis_index("dp")
    t = lax.axis_index("tensor")
    z, y = d // ny, d % ny
    nx = nt // 2
    x, c = t // 2, t % 2
    tokens = acts_in.shape[0]
    width = acts_in.shape[1]
    ff = gate_in.shape[1]
    tile = ny * 64

    def at_z(p):
        return {"dp": p * ny + y}

    def at_y(p):
        return {"dp": z * ny + p}

    def slot(xx, cc):
        return (xx % nx) * 2 + cc

    def remote(src, dst, send, recv, where):
        return pltpu.make_async_remote_copy(
            src_ref=src, dst_ref=dst, send_sem=send, recv_sem=recv,
            device_id=where, device_id_type=pl.DeviceIdType.MESH)

    loads = [
        pltpu.make_async_copy(src, dst, load_sem.at[i])
        for i, (src, dst) in enumerate([
            (warm_in.at[0, 0], warm.at[0, z, y]), (warm_in.at[1, 0], warm.at[1, z, y]),
            (gate_in, gate), (up_in, up), (hg_in, hg),
            (acts_in, acts.at[t]), (cot_in, cot.at[t])])
    ]
    for load in loads:
        load.start()

    barrier = pltpu.get_barrier_semaphore()
    to_right = {"tensor": slot(x + 1, c)}
    to_left = {"tensor": slot(x + nx - 1, c)}
    to_twin = {"tensor": slot(x, 1 - c)}

    def greet(where):
        pl.semaphore_signal(barrier, inc=1, device_id=where, device_id_type=pl.DeviceIdType.MESH)

    for where in (to_right, to_left, to_twin):
        greet(where)
    for k in range(1, nz):
        greet(at_z((z + k) % nz))
    for k in range(1, ny):
        greet(at_y((y + k) % ny))
    for load in loads[:2]:
        load.wait()
    pl.semaphore_wait(barrier, 3 + nz - 1 + ny - 1)

    def exchange(n, me, place, src, dst, send, recv):
        for k in range(1, n):
            to = (me + k) % n
            remote(src(to), dst(k, me), send.at[k - 1], recv.at[k - 1], place(to)).start()

    def landed(n, me, place, src, dst, send, recv, k):
        owner = (me + n - k) % n
        return remote(src(owner), dst(k, owner), send.at[k - 1], recv.at[k - 1], place(owner))

    def first_phase(which, pieces):
        plans = []
        for i, (along_y, block) in enumerate(pieces):
            if along_y:
                plan = (ny, y, at_y, lambda to, b=block: b(z, y), lambda k, o, b=block: b(z, o))
            else:
                plan = (nz, z, at_z, lambda to, b=block: b(z, y), lambda k, o, b=block: b(o, y))
            plans.append(plan + (first_send.at[which, i], first_recv.at[which, i]))
        return plans

    def start_first(plans):
        for plan in plans:
            exchange(*plan)

    def wait_first(plans):
        for plan in plans:
            for k in range(1, plan[0]):
                landed(*plan, k).wait_recv()

    def drain_first(plans):
        for plan in plans:
            for k in range(1, plan[0]):
                landed(*plan, k).wait_send()

    def ring_copies(streams, step, half, i, receiving):
        n, me, place, pieces, turn, which = streams[i]
        if receiving:
            block = (me + n - turn * (1 + step)) % n
        else:
            block = (me + n - turn * step) % n
        to = (me + n + turn) % n
        return [
            remote(ref, ref, ring_send.at[which, i, step, half, j],
                   ring_recv.at[which, i, step, half, j], place(to))
            for j, ref in enumerate(pieces(block, half))
        ]

    def ring_moves(n, turn, step):
        if step < n // 2 - 1:
            return (0, 1) if turn > 0 else (1, 0)
        return (0,) if turn > 0 else (1,)

    def ring_start(streams):
        for order in range(2):
            for i, (n, _, _, _, turn, _) in enumerate(streams):
                halves = ring_moves(n, turn, 0)
                if order < len(halves):
                    for copy in ring_copies(streams, 0, halves[order], i, False):
                        copy.start()

    def ring_advance(streams, step):
        for order in range(2):
            for i, (n, _, _, _, turn, _) in enumerate(streams):
                if step >= n // 2:
                    continue
                halves = ring_moves(n, turn, step)
                if order < len(halves):
                    half = halves[order]
                    for copy in ring_copies(streams, step, half, i, True):
                        copy.wait_recv()
                    if step + 1 < n // 2 and half in ring_moves(n, turn, step + 1):
                        for copy in ring_copies(streams, step + 1, half, i, False):
                            copy.start()

    def ring_drain(streams):
        for i, (n, _, _, _, turn, _) in enumerate(streams):
            for step in range(n // 2):
                for half in ring_moves(n, turn, step):
                    for copy in ring_copies(streams, step, half, i, False):
                        copy.wait_send()

    def ring_streams(which, z_pieces, y_pieces):
        return [
            (nz, z, at_z, z_pieces, 1, which), (nz, z, at_z, z_pieces, -1, which),
            (ny, y, at_y, y_pieces, 1, which), (ny, y, at_y, y_pieces, -1, which)]

    here = slot(x, c)
    behind, ahead, across = slot(x + nx - 1, c), slot(x + 1, c), slot(x + 2, c)
    twin = [slot(x, 1 - c), slot(x + nx - 1, 1 - c), slot(x + 1, 1 - c), slot(x + 2, 1 - c)]
    tok_sends = []

    def tok(i, src, dst, where):
        copy = remote(src, dst, tok_send.at[i], tok_recv.at[i], where)
        copy.start()
        tok_sends.append(copy)

    def tok_wait(i, ref):
        remote(ref, ref, tok_send.at[i], tok_recv.at[i], to_twin).wait_recv()

    warm_first = first_phase(0, [
        (True, lambda zz, yy: warm.at[0, zz, yy]), (False, lambda zz, yy: warm.at[1, zz, yy])])
    start_first(warm_first)
    tok(0, acts_in, acts.at[here], to_right)
    tok(3, cot_in, cot.at[here], to_left)
    tok(1, cot_in, cot.at[here], to_right)
    tok(2, acts_in, acts.at[here], to_left)
    tok(6, acts_in, acts.at[here], to_twin)
    tok(10, cot_in, cot.at[here], to_twin)

    for load in loads[2:5]:
        load.wait()

    def backward(i, carry):
        rows = pl.ds(pl.multiple_of(i * 16, 16), 16)
        gate_w = gate[rows, :].astype(F32)
        up_w = up[rows, :].astype(F32)
        hg_w = hg[rows, :].astype(F32)
        sigma = jax.nn.sigmoid(gate_w)
        active = gate_w * sigma
        hidden[rows, :] = (active * up_w).astype(BF16)
        gate_back[rows, :] = (hg_w * up_w * sigma * (1.0 + gate_w * (1.0 - sigma))).astype(BF16)
        up_back[rows, :] = (hg_w * active).astype(BF16)
        return carry

    steps = gate_in.shape[0] // 16
    lax.fori_loop(0, steps // 2, backward, 0)

    wait_first(warm_first)
    halves_y, halves_z = ny // 2, nz // 2
    warm_ring = ring_streams(
        0,
        lambda b, h: [warm.at[0, b, pl.ds(h * halves_y, halves_y)]],
        lambda b, h: [warm.at[1, pl.ds(h * halves_z, halves_z), b]])
    ring_start(warm_ring)
    lax.fori_loop(steps // 2, steps, backward, 0)

    tok_wait(0, acts.at[behind])
    tok(4, acts.at[behind], acts.at[behind], to_right)
    tok(7, acts.at[behind], acts.at[behind], to_twin)
    tok_wait(3, cot.at[ahead])
    tok(5, cot.at[ahead], cot.at[ahead], to_left)
    tok(12, cot.at[ahead], cot.at[ahead], to_twin)
    ring_advance(warm_ring, 0)
    tok_wait(2, acts.at[ahead])
    tok(8, acts.at[ahead], acts.at[ahead], to_twin)
    tok_wait(1, cot.at[behind])
    tok(11, cot.at[behind], cot.at[behind], to_twin)
    for step in range(1, max(nz, ny) // 2):
        ring_advance(warm_ring, step)
    tok_wait(4, acts.at[across])
    tok(9, acts.at[across], acts.at[across], to_twin)
    tok_wait(5, cot.at[across])
    tok(13, cot.at[across], cot.at[across], to_twin)
    for load in loads[5:]:
        load.wait()
    for i in range(4):
        tok_wait(6 + i, acts.at[twin[i]])
        tok_wait(10 + i, cot.at[twin[i]])

    def probe(tokens_ref, w):
        def body(i, total):
            columns = pl.ds(pl.multiple_of(i * tile, tile), tile)
            rows = tokens_ref[:, :, columns].reshape(nt * tokens, tile)
            factor = two_halves(warm[w, i].reshape(tile, RANK))
            return total + jnp.dot(rows, factor, preferred_element_type=F32)

        pair = lax.fori_loop(0, nz, body, jnp.zeros((nt * tokens, 2 * RANK), F32))
        return two_halves(pair[:, :RANK] + pair[:, RANK:])

    probe_u = probe(acts, 0)
    probe_d = probe(cot, 1)

    def folded(pair):
        return (pair[:, :RANK] + pair[:, RANK:]).astype(BF16)

    per_tile = ff // tile

    def raw_tile(source, first):
        def body(i, carry):
            columns = pl.ds(pl.multiple_of(i * tile, tile), tile)
            block = folded(tdot(source[:, columns], probe_u)).reshape(ny, 64, RANK)
            part_a[first + i] = block[:, :CUT]
            part_b[first + i, :, :64 - CUT] = block[:, CUT:]
            return carry
        return body

    lax.fori_loop(0, per_tile, raw_tile(gate_back, 0), 0)
    lax.fori_loop(0, per_tile, raw_tile(up_back, per_tile), 0)

    sends = []

    def start_one(i, a, b, ga, gb):
        plans = [
            (nz, z, at_z, lambda to: a.at[to], lambda k, o: ga.at[k - 1], one_send.at[i, 0], one_recv.at[i, 0]),
            (ny, y, at_y, lambda to: b.at[:, to], lambda k, o: gb.at[k - 1], one_send.at[i, 1], one_recv.at[i, 1])]
        return plans

    raw_one = start_one(0, part_a, part_b, got_a, got_b)
    exchange(*raw_one[0])

    def down_tile(i, carry):
        columns = pl.ds(pl.multiple_of(i * tile, tile), tile)
        block = folded(tdot(hidden[:, columns], probe_d)).reshape(2, ny, 32, RANK)
        part_b[pl.ds(2 * i, 2), :, 64 - CUT:] = block
        return carry

    lax.fori_loop(0, per_tile, down_tile, 0)
    exchange(*raw_one[1])

    def scatter_rest(i, plans, a, b, ga, gb, sa, sb, fa, fb, done):
        sa[...] = a[z].astype(F32)
        sb[...] = b[:, y].astype(F32)
        two = [
            (ny, y, at_y, lambda to: sa.at[to], lambda k, o: fa.at[k - 1], two_send.at[i, 0], two_recv.at[i, 0]),
            (nz, z, at_z, lambda to: sb.at[to], lambda k, o: fb.at[k - 1], two_send.at[i, 1], two_recv.at[i, 1])]
        for plan, total, got, second in ((plans[0], sa, ga, two[0]), (plans[1], sb, gb, two[1])):
            for k in range(1, plan[0]):
                landed(*plan, k).wait_recv()
                total[...] += got[k - 1].astype(F32)
            exchange(*second)
        for route, (plan, total, fin, me) in enumerate(((two[0], sa, fa, y), (two[1], sb, fb, z))):
            value = total[me]
            for k in range(1, plan[0]):
                landed(*plan, k).wait_recv()
                value = value + fin[k - 1]
            done(route, value)
        return plans + two

    def raw_done(route, value):
        if route == 0:
            raw_u[:CUT] = value
        else:
            raw_u[CUT:] = value[:64 - CUT]
            raw_d[...] = value[64 - CUT:]

    sent = scatter_rest(0, raw_one, part_a, part_b, got_a, got_b, sum_a, sum_b, fin_a, fin_b, raw_done)

    all_u[z, y] = raw_u[...].astype(BF16)
    all_d[z, y] = raw_d[...].astype(BF16)
    raw_first = first_phase(1, [
        (True, lambda zz, yy: all_u.at[zz, yy, pl.ds(0, CUT)]),
        (False, lambda zz, yy: all_u.at[zz, yy, pl.ds(CUT, 64 - CUT)]),
        (False, lambda zz, yy: all_d.at[zz, yy])])
    start_first(raw_first)
    raw_ring = ring_streams(
        1,
        lambda b, h: [all_u.at[b, pl.ds(h * halves_y, halves_y), pl.ds(0, CUT)]],
        lambda b, h: [
            all_u.at[pl.ds(h * halves_z, halves_z), b, pl.ds(CUT, 64 - CUT)],
            all_d.at[pl.ds(h * halves_z, halves_z), b]])
    wait_first(raw_first)
    ring_start(raw_ring)
    for step in range(max(nz, ny) // 2):
        ring_advance(raw_ring, step)

    flat_u = all_u[...].reshape(2 * ff, RANK)
    mixed_u = two_halves(
        jnp.dot(gate_back[...], flat_u[:ff], preferred_element_type=F32)
        + jnp.dot(up_back[...], flat_u[ff:], preferred_element_type=F32))
    flat_d = all_d[...].reshape(ff, RANK)
    mixed_d = two_halves(jnp.dot(hidden[...], flat_d, preferred_element_type=F32))

    def right_tile(source, mixed, target):
        def body(i, carry):
            columns = pl.ds(pl.multiple_of(i * tile, tile), tile)
            rows = source[:, :, columns].reshape(nt * tokens, tile)
            target[i] = folded(tdot(rows, mixed)).reshape(ny, 64, RANK)
            return carry
        return body

    right_one = start_one(1, rpart_a, rpart_b, rgot_a, rgot_b)
    lax.fori_loop(0, nz, right_tile(acts, mixed_u, rpart_a), 0)
    exchange(*right_one[0])
    lax.fori_loop(0, nz, right_tile(cot, mixed_d, rpart_b), 0)
    exchange(*right_one[1])

    row = lax.broadcasted_iota(jnp.int32, (RANK, RANK), 0)
    col = lax.broadcasted_iota(jnp.int32, (RANK, RANK), 1)
    for i, flat in enumerate((flat_u, flat_d)):
        gram[i, :, :RANK] = tdot(flat, flat)
        gram[i, :, RANK:] = (row == col).astype(F32)
    lane = lax.broadcasted_iota(jnp.int32, (PANEL, RANK), 1)
    sub = lax.broadcasted_iota(jnp.int32, (PANEL, RANK), 0)
    sub_one = lax.broadcasted_iota(jnp.int32, (PANEL, 1), 0)

    def eliminate(b, carry):
        base = pl.multiple_of(b * PANEL, PANEL)
        rows = pl.ds(base, PANEL)
        panels = [gram[i, rows, :] for i in range(2)]
        for j in range(PANEL):
            for i in range(2):
                panel = panels[i]
                column = jnp.sum(
                    jnp.where(lane == base + j, panel[:, :RANK], 0.0), axis=1, keepdims=True)
                factor = jnp.where(sub_one > j, column / column[j:j + 1], 0.0)
                panels[i] = panel - factor * panel[j:j + 1]
        for i in range(2):
            panel = panels[i]
            gram[i, rows, :] = panel
            head = panel[:, :RANK]
            pivots = jnp.sum(jnp.where(lane == base + sub, head, 0.0), axis=1, keepdims=True)
            weights = jnp.where(lane >= base + PANEL, head / pivots, 0.0)
            gram[i] -= lax.dot_general(
                weights, panel, (((0,), (0,)), ((), ())),
                precision=lax.Precision.HIGHEST, preferred_element_type=F32)
        return carry

    lax.fori_loop(0, RANK // PANEL, eliminate, 0)
    inverse = []
    for i in range(2):
        pivots = jnp.sum(jnp.where(row == col, gram[i, :, :RANK], 0.0), axis=1, keepdims=True)
        inverse.append(gram[i, :, RANK:] * lax.rsqrt(pivots))

    def solved(values, i):
        return lax.dot_general(
            values, inverse[i], (((1,), (1,)), ((), ())),
            precision=lax.Precision.HIGHEST, preferred_element_type=F32)

    left_u_out[...] = solved(raw_u[...], 0)
    left_d_out[...] = solved(raw_d[...], 1)

    def right_done(route, value):
        right_out[route] = solved(value, route) * (1.0 / (nz * ny))

    sent += scatter_rest(
        1, right_one, rpart_a, rpart_b, rgot_a, rgot_b, rsum_a, rsum_b, rfin_a, rfin_b, right_done)

    for copy in tok_sends:
        copy.wait_send()
    drain_first(warm_first + raw_first + sent)
    ring_drain(warm_ring)
    ring_drain(raw_ring)


def on_device(shape, activations, cotangent, gate_pre, up_value, hidden_grad, warm_factors):
    nz, ny, nt = shape
    tokens, width = activations.shape
    rows, ff = gate_pre.shape
    cut_b = 96 - CUT
    half = max(nz, ny) // 2
    out = pl.pallas_call(
        functools.partial(kernel, nz, ny, nt),
        out_shape=(
            jax.ShapeDtypeStruct((64, RANK), F32),
            jax.ShapeDtypeStruct((32, RANK), F32),
            jax.ShapeDtypeStruct((2, 64, RANK), F32)),
        in_specs=[pl.BlockSpec(memory_space=pl.ANY)] * 6,
        out_specs=[pl.BlockSpec(memory_space=pltpu.VMEM)] * 3,
        scratch_shapes=[
            pltpu.VMEM((nt, tokens, width), BF16),
            pltpu.VMEM((nt, tokens, width), BF16),
            pltpu.VMEM((rows, ff), BF16),
            pltpu.VMEM((rows, ff), BF16),
            pltpu.VMEM((rows, ff), BF16),
            pltpu.VMEM((2, nz, ny, 64, RANK), F32),
            pltpu.VMEM((rows, ff), BF16),
            pltpu.VMEM((rows, ff), BF16),
            pltpu.VMEM((rows, ff), BF16),
            pltpu.VMEM((nz, ny, CUT, RANK), BF16),
            pltpu.VMEM((nz, ny, cut_b, RANK), BF16),
            pltpu.VMEM((nz - 1, ny, CUT, RANK), BF16),
            pltpu.VMEM((ny - 1, nz, cut_b, RANK), BF16),
            pltpu.VMEM((ny, CUT, RANK), F32),
            pltpu.VMEM((nz, cut_b, RANK), F32),
            pltpu.VMEM((ny - 1, CUT, RANK), F32),
            pltpu.VMEM((nz - 1, cut_b, RANK), F32),
            pltpu.VMEM((64, RANK), F32),
            pltpu.VMEM((32, RANK), F32),
            pltpu.VMEM((nz, ny, 64, RANK), BF16),
            pltpu.VMEM((nz, ny, 32, RANK), BF16),
            pltpu.VMEM((nz, ny, 64, RANK), BF16),
            pltpu.VMEM((nz, ny, 64, RANK), BF16),
            pltpu.VMEM((nz - 1, ny, 64, RANK), BF16),
            pltpu.VMEM((ny - 1, nz, 64, RANK), BF16),
            pltpu.VMEM((ny, 64, RANK), F32),
            pltpu.VMEM((nz, 64, RANK), F32),
            pltpu.VMEM((ny - 1, 64, RANK), F32),
            pltpu.VMEM((nz - 1, 64, RANK), F32),
            pltpu.VMEM((2, RANK, 2 * RANK), F32),
            pltpu.SemaphoreType.DMA((7,)),
            pltpu.SemaphoreType.DMA((14,)),
            pltpu.SemaphoreType.DMA((14,)),
            pltpu.SemaphoreType.DMA((2, 3, max(nz, ny) - 1)),
            pltpu.SemaphoreType.DMA((2, 3, max(nz, ny) - 1)),
            pltpu.SemaphoreType.DMA((2, 4, half, 2, 2)),
            pltpu.SemaphoreType.DMA((2, 4, half, 2, 2)),
            pltpu.SemaphoreType.DMA((2, 2, max(nz, ny) - 1)),
            pltpu.SemaphoreType.DMA((2, 2, max(nz, ny) - 1)),
            pltpu.SemaphoreType.DMA((2, 2, max(nz, ny) - 1)),
            pltpu.SemaphoreType.DMA((2, 2, max(nz, ny) - 1)),
        ],
        compiler_params=pltpu.CompilerParams(
            collective_id=0, has_side_effects=True, vmem_limit_bytes=56 * 1024 * 1024),
        name="powersgd_step",
    )(activations, cotangent, gate_pre, up_value, hidden_grad, warm_factors)
    left_united, left_down, right = out
    return left_united[None], left_down[None], right[:, None]


def solution(mesh):
    dp, nt = mesh.shape["dp"], mesh.shape["tensor"]
    ny = 1 << (dp.bit_length() // 2)
    in_specs = (
        P(("dp", "tensor"), None),
        P(("dp", "tensor"), None),
        P("dp", "tensor"),
        P("dp", "tensor"),
        P("dp", "tensor"),
        P(None, "tensor", "dp", None),
    )
    out_specs = (P("tensor", "dp", None), P("tensor", "dp", None), P(None, "tensor", "dp", None))
    return jax.shard_map(
        functools.partial(on_device, (dp // ny, ny, nt)),
        mesh=mesh, in_specs=in_specs, out_specs=out_specs, check_vma=False)
```

```python
import functools

import jax
import jax.numpy as jnp
from jax import lax
from jax.experimental import pallas as pl
from jax.experimental.pallas import tpu as pltpu
from jax.sharding import PartitionSpec as P

F32 = jnp.float32
BF16 = jnp.bfloat16
RANK = 128
CUT = 48
FINE = 32
PANEL = 16


def tdot(left, right):
    return lax.dot_general(left, right, (((0,), (0,)), ((), ())), preferred_element_type=F32)


def two_halves(values):
    high = values.astype(BF16)
    low = (values - high.astype(F32)).astype(BF16)
    return jnp.concatenate([high, low], axis=1)


def kernel(nz, ny, nt, acts_in, cot_in, gate_in, up_in, hg_in, warm_in,
           packed_out,
           acts, cot, gate, up, hg, warm_f, warm, fine,
           united, hidden,
           part_a, part_b, part_d, got_a, got_b, got_d, sum_a, sum_b, fin_a, fin_b,
           raw_u, raw_d, all_u, all_d,
           rpart_a, rpart_b, rgot_a, rgot_b, rsum_a, rsum_b, rfin_a, rfin_b,
           gram,
           load_sem, tok_send, tok_recv, first_send, first_recv,
           ring_send, ring_recv, one_send, one_recv, two_send, two_recv):
    d = lax.axis_index("dp")
    t = lax.axis_index("tensor")
    z, y = d // ny, d % ny
    nx = nt // 2
    x, c = t // 2, t % 2
    tokens = acts_in.shape[0]
    width = acts_in.shape[1]
    ff = gate_in.shape[1]
    tile = ny * 64

    def at_z(p):
        return {"dp": p * ny + y}

    def at_y(p):
        return {"dp": z * ny + p}

    def slot(xx, cc):
        return (xx % nx) * 2 + cc

    def remote(src, dst, send, recv, where):
        return pltpu.make_async_remote_copy(
            src_ref=src, dst_ref=dst, send_sem=send, recv_sem=recv,
            device_id=where, device_id_type=pl.DeviceIdType.MESH)

    loads = [
        pltpu.make_async_copy(src, dst, load_sem.at[i])
        for i, (src, dst) in enumerate([
            (warm_in, warm_f), (gate_in, gate), (up_in, up), (hg_in, hg),
            (acts_in, acts.at[t]), (cot_in, cot.at[t])])
    ]
    for load in loads:
        load.start()

    barrier = pltpu.get_barrier_semaphore()
    to_right = {"tensor": slot(x + 1, c)}
    to_left = {"tensor": slot(x + nx - 1, c)}
    to_twin = {"tensor": slot(x, 1 - c)}

    def greet(where):
        pl.semaphore_signal(barrier, inc=1, device_id=where, device_id_type=pl.DeviceIdType.MESH)

    for where in (to_right, to_left, to_twin):
        greet(where)
    for k in range(1, nz):
        greet(at_z((z + k) % nz))
    for k in range(1, ny):
        greet(at_y((y + k) % ny))
    loads[0].wait()
    coarse = 64 - FINE
    fine[:, :, :, :coarse] = jnp.zeros((2, nz, ny, coarse, RANK), BF16)
    for w in range(2):
        values = warm_f[w, 0]
        high = values.astype(BF16)
        warm[w, z, y] = high
        fine[w, z, y, coarse:] = (values - high.astype(F32)).astype(BF16)[coarse:]
    pl.semaphore_wait(barrier, 3 + nz - 1 + ny - 1)

    def exchange(n, me, place, src, dst, send, recv):
        for k in range(1, n):
            to = (me + k) % n
            remote(src(to), dst(k, me), send.at[k - 1], recv.at[k - 1], place(to)).start()

    def landed(n, me, place, src, dst, send, recv, k):
        owner = (me + n - k) % n
        return remote(src(owner), dst(k, owner), send.at[k - 1], recv.at[k - 1], place(owner))

    def first_phase(which, pieces):
        plans = []
        for i, (along_y, block) in enumerate(pieces):
            if along_y:
                plan = (ny, y, at_y, lambda to, b=block: b(z, y), lambda k, o, b=block: b(z, o))
            else:
                plan = (nz, z, at_z, lambda to, b=block: b(z, y), lambda k, o, b=block: b(o, y))
            plans.append(plan + (first_send.at[which, i], first_recv.at[which, i]))
        return plans

    def start_first(plans):
        for plan in plans:
            exchange(*plan)

    def wait_first(plans):
        for plan in plans:
            for k in range(1, plan[0]):
                landed(*plan, k).wait_recv()

    def drain_first(plans):
        for plan in plans:
            for k in range(1, plan[0]):
                landed(*plan, k).wait_send()

    def ring_copies(streams, step, half, i, receiving):
        n, me, place, pieces, turn, which = streams[i]
        if receiving:
            block = (me + n - turn * (1 + step)) % n
        else:
            block = (me + n - turn * step) % n
        to = (me + n + turn) % n
        return [
            remote(ref, ref, ring_send.at[which, i, step, half, j],
                   ring_recv.at[which, i, step, half, j], place(to))
            for j, ref in enumerate(pieces(block, half))
        ]

    def ring_moves(n, turn, step):
        if step < n // 2 - 1:
            return (0, 1) if turn > 0 else (1, 0)
        return (0,) if turn > 0 else (1,)

    def ring_start(streams):
        for order in range(2):
            for i, (n, _, _, _, turn, _) in enumerate(streams):
                halves = ring_moves(n, turn, 0)
                if order < len(halves):
                    for copy in ring_copies(streams, 0, halves[order], i, False):
                        copy.start()

    def ring_advance(streams, step):
        for order in range(2):
            for i, (n, _, _, _, turn, _) in enumerate(streams):
                if step >= n // 2:
                    continue
                halves = ring_moves(n, turn, step)
                if order < len(halves):
                    half = halves[order]
                    for copy in ring_copies(streams, step, half, i, True):
                        copy.wait_recv()
                    if step + 1 < n // 2 and half in ring_moves(n, turn, step + 1):
                        for copy in ring_copies(streams, step + 1, half, i, False):
                            copy.start()

    def ring_drain(streams):
        for i, (n, _, _, _, turn, _) in enumerate(streams):
            for step in range(n // 2):
                for half in ring_moves(n, turn, step):
                    for copy in ring_copies(streams, step, half, i, False):
                        copy.wait_send()

    def ring_streams(which, z_pieces, y_pieces):
        return [
            (nz, z, at_z, z_pieces, 1, which), (nz, z, at_z, z_pieces, -1, which),
            (ny, y, at_y, y_pieces, 1, which), (ny, y, at_y, y_pieces, -1, which)]

    here = slot(x, c)
    behind, ahead, across = slot(x + nx - 1, c), slot(x + 1, c), slot(x + 2, c)
    twin = [slot(x, 1 - c), slot(x + nx - 1, 1 - c), slot(x + 1, 1 - c), slot(x + 2, 1 - c)]
    tok_sends = []

    def tok(i, src, dst, where):
        copy = remote(src, dst, tok_send.at[i], tok_recv.at[i], where)
        copy.start()
        tok_sends.append(copy)

    def tok_wait(i, ref):
        remote(ref, ref, tok_send.at[i], tok_recv.at[i], to_twin).wait_recv()

    def slow(w, zz, yy):
        return fine.at[w, zz, yy, pl.ds(coarse, FINE)]

    warm_first = first_phase(0, [
        (True, lambda zz, yy: warm.at[0, zz, yy]), (False, lambda zz, yy: warm.at[1, zz, yy])])
    fine_first = first_phase(2, [
        (True, lambda zz, yy: slow(0, zz, yy)), (False, lambda zz, yy: slow(1, zz, yy))])
    start_first(warm_first)
    start_first(fine_first)
    tok(0, acts_in, acts.at[here], to_right)
    tok(3, cot_in, cot.at[here], to_left)
    tok(1, cot_in, cot.at[here], to_right)
    tok(2, acts_in, acts.at[here], to_left)
    tok(6, acts_in, acts.at[here], to_twin)
    tok(10, cot_in, cot.at[here], to_twin)

    for load in loads[1:4]:
        load.wait()

    def backward(i, carry):
        rows = pl.ds(pl.multiple_of(i * 16, 16), 16)
        gate_w = gate[rows, :].astype(F32)
        up_w = up[rows, :].astype(F32)
        hg_w = hg[rows, :].astype(F32)
        sigma = jax.nn.sigmoid(gate_w)
        active = gate_w * sigma
        hidden[rows, :] = (active * up_w).astype(BF16)
        united[rows, :ff] = (hg_w * up_w * sigma * (1.0 + gate_w * (1.0 - sigma))).astype(BF16)
        united[rows, ff:] = (hg_w * active).astype(BF16)
        return carry

    steps = gate_in.shape[0] // 16
    lax.fori_loop(0, steps // 2, backward, 0)

    wait_first(warm_first)
    halves_y, halves_z = ny // 2, nz // 2
    warm_ring = ring_streams(
        0,
        lambda b, h: [warm.at[0, b, pl.ds(h * halves_y, halves_y)]],
        lambda b, h: [warm.at[1, pl.ds(h * halves_z, halves_z), b]])
    fine_ring = ring_streams(
        2,
        lambda b, h: [fine.at[0, b, pl.ds(h * halves_y, halves_y), pl.ds(coarse, FINE)]],
        lambda b, h: [fine.at[1, pl.ds(h * halves_z, halves_z), b, pl.ds(coarse, FINE)]])
    ring_start(warm_ring)
    wait_first(fine_first)
    ring_start(fine_ring)
    lax.fori_loop(steps // 2, steps, backward, 0)

    tok_wait(0, acts.at[behind])
    tok(4, acts.at[behind], acts.at[behind], to_right)
    tok(7, acts.at[behind], acts.at[behind], to_twin)
    tok_wait(3, cot.at[ahead])
    tok(5, cot.at[ahead], cot.at[ahead], to_left)
    tok(12, cot.at[ahead], cot.at[ahead], to_twin)
    ring_advance(warm_ring, 0)
    ring_advance(fine_ring, 0)
    tok_wait(2, acts.at[ahead])
    tok(8, acts.at[ahead], acts.at[ahead], to_twin)
    tok_wait(1, cot.at[behind])
    tok(11, cot.at[behind], cot.at[behind], to_twin)
    for step in range(1, max(nz, ny) // 2):
        ring_advance(warm_ring, step)
        ring_advance(fine_ring, step)
    tok_wait(4, acts.at[across])
    tok(9, acts.at[across], acts.at[across], to_twin)
    tok_wait(5, cot.at[across])
    tok(13, cot.at[across], cot.at[across], to_twin)
    for load in loads[4:]:
        load.wait()
    for i in range(4):
        tok_wait(6 + i, acts.at[twin[i]])
        tok_wait(10 + i, cot.at[twin[i]])

    def probe(tokens_ref, w):
        def body(i, total):
            columns = pl.ds(pl.multiple_of(i * tile, tile), tile)
            rows = tokens_ref[:, :, columns].reshape(nt * tokens, tile)
            factor = jnp.concatenate(
                [warm[w, i].reshape(tile, RANK), fine[w, i].reshape(tile, RANK)], axis=1)
            return total + jnp.dot(rows, factor, preferred_element_type=F32)

        pair = lax.fori_loop(0, nz, body, jnp.zeros((nt * tokens, 2 * RANK), F32))
        return two_halves(pair[:, :RANK] + pair[:, RANK:])

    def folded(pair):
        return (pair[:, :RANK] + pair[:, RANK:]).astype(BF16)

    def along_z(i, j, a, ga):
        return (nz, z, at_z, lambda to: a.at[to], lambda k, o: ga.at[k - 1],
                one_send.at[i, j], one_recv.at[i, j])

    def along_y(i, j, b, gb):
        return (ny, y, at_y, lambda to: b.at[:, to], lambda k, o: gb.at[k - 1],
                one_send.at[i, j], one_recv.at[i, j])

    def send_one(plan, k):
        n, me, place, src, dst, send, recv = plan
        to = (me + k) % n
        remote(src(to), dst(k, me), send.at[k - 1], recv.at[k - 1], place(to)).start()

    plan_a = along_z(0, 0, part_a, got_a)
    plan_d = along_y(0, 1, part_d, got_d)
    plan_b = along_y(0, 2, part_b, got_b)

    probe_d = probe(cot, 1)

    def down_tile(i, carry):
        columns = pl.ds(pl.multiple_of(i * tile, tile), tile)
        block = folded(tdot(hidden[:, columns], probe_d)).reshape(2, ny, 32, RANK)
        part_d[pl.ds(2 * i, 2)] = block
        return carry

    lax.fori_loop(0, ff // tile, down_tile, 0)
    exchange(*plan_d)

    probe_u = probe(acts, 0)

    def united_tile(k, carry):
        i = (z + k) % nz
        columns = pl.ds(pl.multiple_of(i * tile, tile), tile)
        block = folded(tdot(united[:, columns], probe_u)).reshape(ny, 64, RANK)
        part_a[i] = block[:, :CUT]
        part_b[i] = block[:, CUT:]

        @pl.when(k < nz)
        def _():
            send_one(plan_a, k)
        return carry

    lax.fori_loop(1, nz + 1, united_tile, 0)
    exchange(*plan_b)

    def scatter_rest(i, firsts_a, firsts_b, sa, sb, fa, fb, done):
        two = [
            (ny, y, at_y, lambda to: sa.at[to], lambda k, o: fa.at[k - 1], two_send.at[i, 0], two_recv.at[i, 0]),
            (nz, z, at_z, lambda to: sb.at[to], lambda k, o: fb.at[k - 1], two_send.at[i, 1], two_recv.at[i, 1])]
        for firsts, second in ((firsts_a, two[0]), (firsts_b, two[1])):
            for plan, own, total, got in firsts:
                total[...] = own[...].astype(F32)
                for k in range(1, plan[0]):
                    landed(*plan, k).wait_recv()
                    total[...] += got[k - 1].astype(F32)
            exchange(*second)
        for route, (plan, total, fin, me) in enumerate(((two[0], sa, fa, y), (two[1], sb, fb, z))):
            value = total[me]
            for k in range(1, plan[0]):
                landed(*plan, k).wait_recv()
                value = value + fin[k - 1]
            done(route, value)
        return two

    def raw_done(route, value):
        if route == 0:
            raw_u[:CUT] = value
        else:
            raw_u[CUT:] = value[:64 - CUT]
            raw_d[...] = value[64 - CUT:]

    raw_two = scatter_rest(
        0, [(plan_a, part_a.at[z], sum_a, got_a)],
        [(plan_d, part_d.at[:, y], sum_b.at[:, pl.ds(64 - CUT, 32)], got_d),
         (plan_b, part_b.at[:, y], sum_b.at[:, pl.ds(0, 64 - CUT)], got_b)],
        sum_a, sum_b, fin_a, fin_b, raw_done)

    all_u[z, y] = raw_u[...].astype(BF16)
    all_d[z, y] = raw_d[...].astype(BF16)
    raw_first = first_phase(1, [
        (True, lambda zz, yy: all_u.at[zz, yy, pl.ds(0, CUT)]),
        (False, lambda zz, yy: all_u.at[zz, yy, pl.ds(CUT, 64 - CUT)]),
        (False, lambda zz, yy: all_d.at[zz, yy])])
    start_first(raw_first)
    raw_ring = ring_streams(
        1,
        lambda b, h: [all_u.at[b, pl.ds(h * halves_y, halves_y), pl.ds(0, CUT)]],
        lambda b, h: [
            all_u.at[pl.ds(h * halves_z, halves_z), b, pl.ds(CUT, 64 - CUT)],
            all_d.at[pl.ds(h * halves_z, halves_z), b]])
    wait_first(raw_first)
    ring_start(raw_ring)
    for step in range(max(nz, ny) // 2):
        ring_advance(raw_ring, step)

    flat_u = all_u[...].reshape(2 * ff, RANK)
    mixed_u = two_halves(jnp.dot(united[...], flat_u, preferred_element_type=F32))
    flat_d = all_d[...].reshape(ff, RANK)
    mixed_d = two_halves(jnp.dot(hidden[...], flat_d, preferred_element_type=F32))
    rplan_a = along_z(1, 0, rpart_a, rgot_a)
    rplan_b = along_y(1, 1, rpart_b, rgot_b)
    rounds = ny // 2
    per_round = nz // rounds

    def right_round(q, carry):
        for extra in range(per_round):
            k = (q - 1) * per_round + extra + 1
            i = (z + k) % nz
            columns = pl.ds(pl.multiple_of(i * tile, tile), tile)
            rows = acts[:, :, columns].reshape(nt * tokens, tile)
            rpart_a[i] = folded(tdot(rows, mixed_u)).reshape(ny, 64, RANK)

            @pl.when(k < nz)
            def _():
                send_one(rplan_a, k)

        pair = (y // 2 + q) % rounds
        rows = jnp.concatenate(
            [cot[:, :, pl.ds(pl.multiple_of(i * tile + pair * 128, 128), 128)].reshape(
                nt * tokens, 128) for i in range(nz)], axis=1)
        rpart_b[:, pl.ds(2 * pair, 2)] = folded(tdot(rows, mixed_d)).reshape(nz, 2, 64, RANK)
        for extra in range(2):
            to = 2 * pair + extra

            @pl.when(to != y)
            def _():
                send_one(rplan_b, (to + ny - y) % ny)
        return carry

    lax.fori_loop(1, rounds + 1, right_round, 0)

    row = lax.broadcasted_iota(jnp.int32, (RANK, RANK), 0)
    col = lax.broadcasted_iota(jnp.int32, (RANK, RANK), 1)
    for i, flat in enumerate((flat_u, flat_d)):
        gram[i, :, :RANK] = tdot(flat, flat)
        gram[i, :, RANK:] = (row == col).astype(F32)
    lane = lax.broadcasted_iota(jnp.int32, (PANEL, RANK), 1)
    sub = lax.broadcasted_iota(jnp.int32, (PANEL, RANK), 0)
    sub_one = lax.broadcasted_iota(jnp.int32, (PANEL, 1), 0)

    def eliminate(b, carry):
        base = pl.multiple_of(b * PANEL, PANEL)
        rows = pl.ds(base, PANEL)
        panels = [gram[i, rows, :] for i in range(2)]
        for j in range(PANEL):
            for i in range(2):
                panel = panels[i]
                column = jnp.sum(
                    jnp.where(lane == base + j, panel[:, :RANK], 0.0), axis=1, keepdims=True)
                factor = jnp.where(sub_one > j, column / column[j:j + 1], 0.0)
                panels[i] = panel - factor * panel[j:j + 1]
        for i in range(2):
            panel = panels[i]
            gram[i, rows, :] = panel
            head = panel[:, :RANK]
            pivots = jnp.sum(jnp.where(lane == base + sub, head, 0.0), axis=1, keepdims=True)
            weights = jnp.where(lane >= base + PANEL, head / pivots, 0.0)
            gram[i] -= lax.dot_general(
                weights, panel, (((0,), (0,)), ((), ())),
                precision=lax.Precision.HIGHEST, preferred_element_type=F32)
        return carry

    lax.fori_loop(0, RANK // PANEL, eliminate, 0)
    inverse = []
    for i in range(2):
        pivots = jnp.sum(jnp.where(row == col, gram[i, :, :RANK], 0.0), axis=1, keepdims=True)
        inverse.append(gram[i, :, RANK:] * lax.rsqrt(pivots))

    def solved(values, i):
        return lax.dot_general(
            values, inverse[i], (((1,), (1,)), ((), ())),
            precision=lax.Precision.HIGHEST, preferred_element_type=F32)

    packed_out[:64] = solved(raw_u[...], 0)
    packed_out[64:96] = solved(raw_d[...], 1)

    for copy in tok_sends:
        copy.wait_send()
    drain_first(warm_first + fine_first + raw_first + [plan_a, plan_d, plan_b] + raw_two)
    for ring in (warm_ring, fine_ring, raw_ring):
        ring_drain(ring)

    def right_done(route, value):
        packed_out[96 + 64 * route:160 + 64 * route] = solved(value, route) * (1.0 / (nz * ny))

    right_two = scatter_rest(
        1, [(rplan_a, rpart_a.at[z], rsum_a, rgot_a)], [(rplan_b, rpart_b.at[:, y], rsum_b, rgot_b)],
        rsum_a, rsum_b, rfin_a, rfin_b, right_done)
    drain_first([rplan_a, rplan_b] + right_two)


def unpack(packed, left_u, left_d, right):
    left_u[...] = packed[:64]
    left_d[...] = packed[64:96]
    right[0] = packed[96:160]
    right[1] = packed[160:224]


def on_device(shape, activations, cotangent, gate_pre, up_value, hidden_grad, warm_factors):
    nz, ny, nt = shape
    tokens, width = activations.shape
    rows, ff = gate_pre.shape
    cut_b = 96 - CUT
    half = max(nz, ny) // 2
    packed = pl.pallas_call(
        functools.partial(kernel, nz, ny, nt),
        out_shape=jax.ShapeDtypeStruct((224, RANK), F32),
        in_specs=[pl.BlockSpec(memory_space=pl.ANY)] * 6,
        out_specs=pl.BlockSpec(memory_space=pltpu.VMEM),
        scratch_shapes=[
            pltpu.VMEM((nt, tokens, width), BF16),
            pltpu.VMEM((nt, tokens, width), BF16),
            pltpu.VMEM((rows, ff), BF16),
            pltpu.VMEM((rows, ff), BF16),
            pltpu.VMEM((rows, ff), BF16),
            pltpu.VMEM((2, 1, 64, RANK), F32),
            pltpu.VMEM((2, nz, ny, 64, RANK), BF16),
            pltpu.VMEM((2, nz, ny, 64, RANK), BF16),
            pltpu.VMEM((rows, 2 * ff), BF16),
            pltpu.VMEM((rows, ff), BF16),
            pltpu.VMEM((nz, ny, CUT, RANK), BF16),
            pltpu.VMEM((nz, ny, 64 - CUT, RANK), BF16),
            pltpu.VMEM((nz, ny, 32, RANK), BF16),
            pltpu.VMEM((nz - 1, ny, CUT, RANK), BF16),
            pltpu.VMEM((ny - 1, nz, 64 - CUT, RANK), BF16),
            pltpu.VMEM((ny - 1, nz, 32, RANK), BF16),
            pltpu.VMEM((ny, CUT, RANK), F32),
            pltpu.VMEM((nz, cut_b, RANK), F32),
            pltpu.VMEM((ny - 1, CUT, RANK), F32),
            pltpu.VMEM((nz - 1, cut_b, RANK), F32),
            pltpu.VMEM((64, RANK), F32),
            pltpu.VMEM((32, RANK), F32),
            pltpu.VMEM((nz, ny, 64, RANK), BF16),
            pltpu.VMEM((nz, ny, 32, RANK), BF16),
            pltpu.VMEM((nz, ny, 64, RANK), BF16),
            pltpu.VMEM((nz, ny, 64, RANK), BF16),
            pltpu.VMEM((nz - 1, ny, 64, RANK), BF16),
            pltpu.VMEM((ny - 1, nz, 64, RANK), BF16),
            pltpu.VMEM((ny, 64, RANK), F32),
            pltpu.VMEM((nz, 64, RANK), F32),
            pltpu.VMEM((ny - 1, 64, RANK), F32),
            pltpu.VMEM((nz - 1, 64, RANK), F32),
            pltpu.VMEM((2, RANK, 2 * RANK), F32),
            pltpu.SemaphoreType.DMA((6,)),
            pltpu.SemaphoreType.DMA((14,)),
            pltpu.SemaphoreType.DMA((14,)),
            pltpu.SemaphoreType.DMA((3, 3, max(nz, ny) - 1)),
            pltpu.SemaphoreType.DMA((3, 3, max(nz, ny) - 1)),
            pltpu.SemaphoreType.DMA((3, 4, half, 2, 2)),
            pltpu.SemaphoreType.DMA((3, 4, half, 2, 2)),
            pltpu.SemaphoreType.DMA((2, 3, max(nz, ny) - 1)),
            pltpu.SemaphoreType.DMA((2, 3, max(nz, ny) - 1)),
            pltpu.SemaphoreType.DMA((2, 2, max(nz, ny) - 1)),
            pltpu.SemaphoreType.DMA((2, 2, max(nz, ny) - 1)),
        ],
        compiler_params=pltpu.CompilerParams(
            collective_id=0, has_side_effects=True, vmem_limit_bytes=56 * 1024 * 1024),
        name="powersgd_step",
    )(activations, cotangent, gate_pre, up_value, hidden_grad, warm_factors)
    left_united, left_down, right = pl.pallas_call(
        unpack,
        out_shape=(
            jax.ShapeDtypeStruct((64, RANK), F32),
            jax.ShapeDtypeStruct((32, RANK), F32),
            jax.ShapeDtypeStruct((2, 64, RANK), F32)),
        name="unpack",
    )(packed)
    return left_united[None], left_down[None], right[:, None]


def solution(mesh):
    dp, nt = mesh.shape["dp"], mesh.shape["tensor"]
    ny = 1 << (dp.bit_length() // 2)
    in_specs = (
        P(("dp", "tensor"), None),
        P(("dp", "tensor"), None),
        P("dp", "tensor"),
        P("dp", "tensor"),
        P("dp", "tensor"),
        P(None, "tensor", "dp", None),
    )
    out_specs = (P("tensor", "dp", None), P("tensor", "dp", None), P(None, "tensor", "dp", None))
    return jax.shard_map(
        functools.partial(on_device, (dp // ny, ny, nt)),
        mesh=mesh, in_specs=in_specs, out_specs=out_specs, check_vma=False)
```

```python
import functools

import jax
import jax.numpy as jnp
from jax import lax
from jax.experimental import pallas as pl
from jax.experimental.pallas import tpu as pltpu
from jax.sharding import PartitionSpec as P

F32 = jnp.float32
BF16 = jnp.bfloat16
RANK = 128
CUT = 48
FINE = 32
PANEL = 16


def tdot(left, right):
    return lax.dot_general(left, right, (((0,), (0,)), ((), ())), preferred_element_type=F32)


def two_halves(values):
    high = values.astype(BF16)
    low = (values - high.astype(F32)).astype(BF16)
    return jnp.concatenate([high, low], axis=1)


def kernel(nz, ny, nt, acts_in, cot_in, gate_in, up_in, hg_in, warm_in,
           packed_out,
           acts, cot, gate, up, hg, warm_f, warm,
           united, hidden,
           part_a, part_b, part_d, got_a, got_b, got_d, sum_a, sum_b, fin_a, fin_b,
           raw_u, raw_d, everyone,
           rpart_a, rpart_b, rgot_a, rgot_b, rsum_a, rsum_b, rfin_a, rfin_b,
           gram, relay_a, relay_d, relay_b, rrelay_a, rrelay_b, keep_a, rkeep_a,
           load_sem, tok_send, tok_recv, first_send, first_recv,
           ring_send, ring_recv, one_send, one_recv, two_send, two_recv, relay_send, relay_recv):
    d = lax.axis_index("dp")
    t = lax.axis_index("tensor")
    z, y = d // ny, d % ny
    nx = nt // 2
    x, c = t // 2, t % 2
    tokens = acts_in.shape[0]
    width = acts_in.shape[1]
    ff = gate_in.shape[1]
    tile = ny * 64

    def at_z(p):
        return {"dp": p * ny + y}

    def at_y(p):
        return {"dp": z * ny + p}

    def slot(xx, cc):
        return (xx % nx) * 2 + cc

    def remote(src, dst, send, recv, where):
        return pltpu.make_async_remote_copy(
            src_ref=src, dst_ref=dst, send_sem=send, recv_sem=recv,
            device_id=where, device_id_type=pl.DeviceIdType.MESH)

    loads = [
        pltpu.make_async_copy(src, dst, load_sem.at[i])
        for i, (src, dst) in enumerate([
            (warm_in, warm_f), (gate_in, gate), (up_in, up), (hg_in, hg),
            (acts_in, acts.at[t]), (cot_in, cot.at[t])])
    ]
    for load in loads:
        load.start()

    barrier = pltpu.get_barrier_semaphore()
    to_right = {"tensor": slot(x + 1, c)}
    to_left = {"tensor": slot(x + nx - 1, c)}
    to_twin = {"tensor": slot(x, 1 - c)}

    def greet(where):
        pl.semaphore_signal(barrier, inc=1, device_id=where, device_id_type=pl.DeviceIdType.MESH)

    for where in (to_right, to_left, to_twin):
        greet(where)
    for k in range(1, nz):
        greet(at_z((z + k) % nz))
    for k in range(1, ny):
        greet(at_y((y + k) % ny))
    loads[0].wait()
    coarse = 64 - FINE
    for w in range(2):
        values = warm_f[w, 0]
        high = values.astype(BF16)
        warm[w, z, y, :64] = high
        warm[w, z, y, 64:] = (values - high.astype(F32)).astype(BF16)[coarse:]
    pl.semaphore_wait(barrier, 3 + nz - 1 + ny - 1)

    def exchange(n, me, place, src, dst, send, recv):
        for k in range(1, n):
            to = (me + k) % n
            remote(src(to), dst(k, me), send.at[k - 1], recv.at[k - 1], place(to)).start()

    def landed(n, me, place, src, dst, send, recv, k):
        owner = (me + n - k) % n
        return remote(src(owner), dst(k, owner), send.at[k - 1], recv.at[k - 1], place(owner))

    def first_phase(which, pieces):
        plans = []
        for i, (along_y, block) in enumerate(pieces):
            if along_y:
                plan = (ny, y, at_y, lambda to, b=block: b(z, y), lambda k, o, b=block: b(z, o))
            else:
                plan = (nz, z, at_z, lambda to, b=block: b(z, y), lambda k, o, b=block: b(o, y))
            plans.append(plan + (first_send.at[which, i], first_recv.at[which, i]))
        return plans

    def start_first(plans):
        for plan in plans:
            exchange(*plan)

    def wait_first(plans):
        for plan in plans:
            for k in range(1, plan[0]):
                landed(*plan, k).wait_recv()

    def drain_first(plans):
        for plan in plans:
            for k in range(1, plan[0]):
                landed(*plan, k).wait_send()

    def ring_copy(streams, step, half, i, receiving):
        n, me, place, pieces, turn, which = streams[i]
        if receiving:
            block = (me + n - turn * (1 + step)) % n
        else:
            block = (me + n - turn * step) % n
        to = (me + n + turn) % n
        ref = pieces(block, half)
        return remote(ref, ref, ring_send.at[which, i, step, half],
                      ring_recv.at[which, i, step, half], place(to))

    def ring_moves(n, turn, step):
        if step < n // 2 - 1:
            return (0, 1) if turn > 0 else (1, 0)
        return (0,) if turn > 0 else (1,)

    def ring_start(streams):
        for order in range(2):
            for i, (n, _, _, _, turn, _) in enumerate(streams):
                halves = ring_moves(n, turn, 0)
                if order < len(halves):
                    ring_copy(streams, 0, halves[order], i, False).start()

    def ring_advance(streams, step):
        for order in range(2):
            for i, (n, _, _, _, turn, _) in enumerate(streams):
                if step >= n // 2:
                    continue
                halves = ring_moves(n, turn, step)
                if order < len(halves):
                    half = halves[order]
                    ring_copy(streams, step, half, i, True).wait_recv()
                    if step + 1 < n // 2 and half in ring_moves(n, turn, step + 1):
                        ring_copy(streams, step + 1, half, i, False).start()

    def ring_drain(streams):
        for i, (n, _, _, _, turn, _) in enumerate(streams):
            for step in range(n // 2):
                for half in ring_moves(n, turn, step):
                    ring_copy(streams, step, half, i, False).wait_send()

    def ring_streams(which, z_pieces, y_pieces):
        return [
            (nz, z, at_z, z_pieces, 1, which), (nz, z, at_z, z_pieces, -1, which),
            (ny, y, at_y, y_pieces, 1, which), (ny, y, at_y, y_pieces, -1, which)]

    here = slot(x, c)
    behind, ahead, across = slot(x + nx - 1, c), slot(x + 1, c), slot(x + 2, c)
    twin = [slot(x, 1 - c), slot(x + nx - 1, 1 - c), slot(x + 1, 1 - c), slot(x + 2, 1 - c)]
    tok_sends = []

    def tok(i, src, dst, where):
        copy = remote(src, dst, tok_send.at[i], tok_recv.at[i], where)
        copy.start()
        tok_sends.append(copy)

    def tok_wait(i, ref):
        remote(ref, ref, tok_send.at[i], tok_recv.at[i], to_twin).wait_recv()

    warm_first = first_phase(0, [
        (True, lambda zz, yy: warm.at[0, zz, yy]), (False, lambda zz, yy: warm.at[1, zz, yy])])
    start_first(warm_first)
    tok(0, acts_in, acts.at[here], to_right)
    tok(3, cot_in, cot.at[here], to_left)
    tok(1, cot_in, cot.at[here], to_right)
    tok(2, acts_in, acts.at[here], to_left)
    tok(6, acts_in, acts.at[here], to_twin)
    tok(10, cot_in, cot.at[here], to_twin)

    for load in loads[1:4]:
        load.wait()

    def backward(i, carry):
        rows = pl.ds(pl.multiple_of(i * 16, 16), 16)
        gate_w = gate[rows, :].astype(F32)
        up_w = up[rows, :].astype(F32)
        hg_w = hg[rows, :].astype(F32)
        sigma = jax.nn.sigmoid(gate_w)
        active = gate_w * sigma
        hidden[rows, :] = (active * up_w).astype(BF16)
        united[rows, :ff] = (hg_w * up_w * sigma * (1.0 + gate_w * (1.0 - sigma))).astype(BF16)
        united[rows, ff:] = (hg_w * active).astype(BF16)
        return carry

    steps = gate_in.shape[0] // 16
    lax.fori_loop(0, steps // 2, backward, 0)

    wait_first(warm_first)
    halves_y, halves_z = ny // 2, nz // 2
    warm_ring = ring_streams(
        0,
        lambda b, h: warm.at[0, b, pl.ds(h * halves_y, halves_y)],
        lambda b, h: warm.at[1, pl.ds(h * halves_z, halves_z), b])
    ring_start(warm_ring)
    lax.fori_loop(steps // 2, steps, backward, 0)

    tok_wait(0, acts.at[behind])
    tok(4, acts.at[behind], acts.at[behind], to_right)
    tok(7, acts.at[behind], acts.at[behind], to_twin)
    tok_wait(3, cot.at[ahead])
    tok(5, cot.at[ahead], cot.at[ahead], to_left)
    tok(12, cot.at[ahead], cot.at[ahead], to_twin)
    ring_advance(warm_ring, 0)
    tok_wait(2, acts.at[ahead])
    tok(8, acts.at[ahead], acts.at[ahead], to_twin)
    tok_wait(1, cot.at[behind])
    tok(11, cot.at[behind], cot.at[behind], to_twin)
    for step in range(1, max(nz, ny) // 2):
        ring_advance(warm_ring, step)
    tok_wait(4, acts.at[across])
    tok(9, acts.at[across], acts.at[across], to_twin)
    tok_wait(5, cot.at[across])
    tok(13, cot.at[across], cot.at[across], to_twin)
    for load in loads[4:]:
        load.wait()
    for i in range(4):
        tok_wait(6 + i, acts.at[twin[i]])
        tok_wait(10 + i, cot.at[twin[i]])

    no_fine = jnp.zeros((ny, coarse, RANK), BF16)

    def probe(tokens_ref, w):
        def body(i, total):
            columns = pl.ds(pl.multiple_of(i * tile, tile), tile)
            rows = tokens_ref[:, :, columns].reshape(nt * tokens, tile)
            factor = jnp.concatenate(
                [warm[w, i, :, :64].reshape(tile, RANK),
                 jnp.concatenate([no_fine, warm[w, i, :, 64:]], axis=1).reshape(tile, RANK)], axis=1)
            return total + jnp.dot(rows, factor, preferred_element_type=F32)

        pair = lax.fori_loop(0, nz, body, jnp.zeros((nt * tokens, 2 * RANK), F32))
        return two_halves(pair[:, :RANK] + pair[:, RANK:])

    def folded(pair):
        return pair[:, :RANK] + pair[:, RANK:]

    def along_z(i, j, a, ga):
        return (nz, z, at_z, lambda to: a.at[to], lambda k, o: ga.at[k - 1],
                one_send.at[i, j], one_recv.at[i, j])

    def along_y(i, j, b, gb):
        return (ny, y, at_y, lambda to: b.at[:, to], lambda k, o: gb.at[k - 1],
                one_send.at[i, j], one_recv.at[i, j])

    def send_one(plan, k):
        n, me, place, src, dst, send, recv = plan
        to = (me + k) % n
        remote(src(to), dst(k, me), send.at[k - 1], recv.at[k - 1], place(to)).start()

    def near(n):
        return [k for k in range(1, n) if abs(k - n // 2) > 1]

    def arriving(n):
        return [k for k in range(1, n) if k != n // 2]

    def is_near(k, n):
        return (k != 0) & (k != n // 2) & (k != n // 2 - 1) & (k != n // 2 + 1)

    def in_order(j, n):
        j = (j + n - 1) % n
        m, odd = (j + 1) // 2, j % 2
        return (odd * m + (1 - odd) * (n - m)) % n

    def relay_copies(plan, r, relay):
        n, me, place, src = plan[:4]
        block = src((me + n // 2) % n)
        size = relay.shape[1]
        return [
            remote(block.at[pl.ds(h * size, size)], relay.at[h], relay_send.at[r, h],
                   relay_recv.at[r, h], place((me + (1, n - 1)[h]) % n)) for h in range(2)]

    def far_out(plan, r, relay):
        for copy in relay_copies(plan, r, relay):
            copy.start()

    def near_out(plan):
        for k in near(plan[0]):
            send_one(plan, k)

    def relayed(plan, r, relay, keep):
        n, me, place, src = plan[:4]
        size = relay.shape[1]
        for h, copy in enumerate(relay_copies(plan, r, relay)):
            copy.wait_recv()
            k = n // 2 - 1 + 2 * h
            piece = src((me + k) % n).at[pl.ds(h * size, size)]
            own = piece if keep is None else keep.at[h, pl.ds(h * size, size)]
            piece[...] = (own[...].astype(F32) + relay[h].astype(F32)).astype(BF16)
            send_one(plan, k)

    def drain_one(plan, r, relay):
        for copy in relay_copies(plan, r, relay):
            copy.wait_send()
        for k in arriving(plan[0]):
            landed(*plan, k).wait_send()

    plan_a = along_z(0, 0, part_a, got_a)
    plan_d = along_y(0, 1, part_d, got_d)
    plan_b = along_y(0, 2, part_b, got_b)

    probe_d = probe(cot, 1)

    def down_tile(i, carry):
        columns = pl.ds(pl.multiple_of(i * tile, tile), tile)
        block = folded(tdot(hidden[:, columns], probe_d)).reshape(2, ny, 32, RANK)
        part_d[pl.ds(2 * i, 2)] = block.astype(BF16)
        return carry

    lax.fori_loop(0, ff // tile, down_tile, 0)
    far_out(plan_d, 1, relay_d)
    near_out(plan_d)

    probe_u = probe(acts, 0)

    def row_out(j, plan, r, relay, keep, total, store, compute):
        k = in_order(j, nz)
        i = (z + k) % nz
        block = folded(compute(pl.ds(pl.multiple_of(i * tile, tile), tile))).reshape(ny, 64, RANK)
        store(i, block.astype(BF16))
        rows = total.shape[1]

        @pl.when(k == 0)
        def _():
            total[...] = block[:, :rows]

        for h in range(2):
            @pl.when(k == nz // 2 - 1 + 2 * h)
            def _():
                keep[h] = block[:, :rows]

        @pl.when(k == nz // 2)
        def _():
            far_out(plan, r, relay)

        @pl.when(is_near(k, nz))
        def _():
            send_one(plan, k)

    def store_raw(i, block):
        part_a[i] = block[:, :CUT]
        part_b[i] = block[:, CUT:]

    def united_tile(j, carry):
        row_out(j, plan_a, 0, relay_a, keep_a, sum_a, store_raw,
                lambda columns: tdot(united[:, columns], probe_u))
        return carry

    lax.fori_loop(0, nz, united_tile, 0)
    far_out(plan_b, 2, relay_b)
    relayed(plan_a, 0, relay_a, keep_a)
    near_out(plan_b)
    relayed(plan_d, 1, relay_d, None)
    relayed(plan_b, 2, relay_b, None)

    def scatter_rest(i, firsts_a, firsts_b, sa, sb, fa, fb, done):
        two = [
            (ny, y, at_y, lambda to: sa.at[to], lambda k, o: fa.at[k - 1], two_send.at[i, 0], two_recv.at[i, 0]),
            (nz, z, at_z, lambda to: sb.at[to], lambda k, o: fb.at[k - 1], two_send.at[i, 1], two_recv.at[i, 1])]
        for firsts, second in ((firsts_a, two[0]), (firsts_b, two[1])):
            for plan, own, total, got in firsts:
                if own is not None:
                    total[...] = own[...].astype(F32)
                for k in arriving(plan[0]):
                    landed(*plan, k).wait_recv()
                    total[...] += got[k - 1].astype(F32)
            exchange(*second)
        for route, (plan, total, fin, me) in enumerate(((two[0], sa, fa, y), (two[1], sb, fb, z))):
            value = total[me]
            for k in range(1, plan[0]):
                landed(*plan, k).wait_recv()
                value = value + fin[k - 1]
            done(route, value)
        return two

    def raw_done(route, value):
        if route == 0:
            raw_u[:CUT] = value
        else:
            raw_u[CUT:] = value[:64 - CUT]
            raw_d[...] = value[64 - CUT:]

    raw_two = scatter_rest(
        0, [(plan_a, None, sum_a, got_a)],
        [(plan_d, part_d.at[:, y], sum_b.at[:, pl.ds(64 - CUT, 32)], got_d),
         (plan_b, part_b.at[:, y], sum_b.at[:, pl.ds(0, 64 - CUT)], got_b)],
        sum_a, sum_b, fin_a, fin_b, raw_done)

    everyone[z, y, :64] = raw_u[...].astype(BF16)
    everyone[z, y, 64:] = raw_d[...].astype(BF16)
    raw_first = first_phase(1, [
        (True, lambda zz, yy: everyone.at[zz, yy, pl.ds(0, CUT)]),
        (False, lambda zz, yy: everyone.at[zz, yy, pl.ds(CUT, 96 - CUT)])])
    start_first(raw_first)
    raw_ring = ring_streams(
        1,
        lambda b, h: everyone.at[b, pl.ds(h * halves_y, halves_y), pl.ds(0, CUT)],
        lambda b, h: everyone.at[pl.ds(h * halves_z, halves_z), b, pl.ds(CUT, 96 - CUT)])
    wait_first(raw_first)
    ring_start(raw_ring)
    for step in range(max(nz, ny) // 2):
        ring_advance(raw_ring, step)

    flat_u = everyone[:, :, :64].reshape(2 * ff, RANK)
    mixed_u = two_halves(jnp.dot(united[...], flat_u, preferred_element_type=F32))
    flat_d = everyone[:, :, 64:].reshape(ff, RANK)
    mixed_d = two_halves(jnp.dot(hidden[...], flat_d, preferred_element_type=F32))
    rplan_a = along_z(1, 0, rpart_a, rgot_a)
    rplan_b = along_y(1, 1, rpart_b, rgot_b)
    rounds = ny // 2
    per_round = nz // rounds

    def store_right(i, block):
        rpart_a[i] = block

    def right_round(q, carry):
        for extra in range(per_round):
            row_out(q * per_round + extra, rplan_a, 3, rrelay_a, rkeep_a, rsum_a, store_right,
                    lambda columns: tdot(acts[:, :, columns].reshape(nt * tokens, tile), mixed_u))

        pair = (y // 2 + q + rounds // 2) % rounds
        rows = jnp.concatenate(
            [cot[:, :, pl.ds(pl.multiple_of(i * tile + pair * 128, 128), 128)].reshape(
                nt * tokens, 128) for i in range(nz)], axis=1)
        rpart_b[:, pl.ds(2 * pair, 2)] = folded(
            tdot(rows, mixed_d)).reshape(nz, 2, 64, RANK).astype(BF16)
        for extra in range(2):
            k = (2 * pair + extra + ny - y) % ny

            @pl.when(k == ny // 2)
            def _():
                far_out(rplan_b, 4, rrelay_b)

            @pl.when(is_near(k, ny))
            def _():
                send_one(rplan_b, k)
        return carry

    lax.fori_loop(0, rounds, right_round, 0)
    relayed(rplan_a, 3, rrelay_a, rkeep_a)
    relayed(rplan_b, 4, rrelay_b, None)

    row = lax.broadcasted_iota(jnp.int32, (RANK, RANK), 0)
    col = lax.broadcasted_iota(jnp.int32, (RANK, RANK), 1)
    for i, flat in enumerate((flat_u, flat_d)):
        gram[i, :, :RANK] = tdot(flat, flat)
        gram[i, :, RANK:] = (row == col).astype(F32)
    lane = lax.broadcasted_iota(jnp.int32, (PANEL, RANK), 1)
    sub = lax.broadcasted_iota(jnp.int32, (PANEL, RANK), 0)
    sub_one = lax.broadcasted_iota(jnp.int32, (PANEL, 1), 0)

    def eliminate(b, carry):
        base = pl.multiple_of(b * PANEL, PANEL)
        rows = pl.ds(base, PANEL)
        panels = [gram[i, rows, :] for i in range(2)]
        for j in range(PANEL):
            for i in range(2):
                panel = panels[i]
                column = jnp.sum(
                    jnp.where(lane == base + j, panel[:, :RANK], 0.0), axis=1, keepdims=True)
                factor = jnp.where(sub_one > j, column / column[j:j + 1], 0.0)
                panels[i] = panel - factor * panel[j:j + 1]
        for i in range(2):
            panel = panels[i]
            gram[i, rows, :] = panel
            head = panel[:, :RANK]
            pivots = jnp.sum(jnp.where(lane == base + sub, head, 0.0), axis=1, keepdims=True)
            weights = jnp.where(lane >= base + PANEL, head / pivots, 0.0)
            gram[i] -= lax.dot_general(
                weights, panel, (((0,), (0,)), ((), ())),
                precision=lax.Precision.HIGHEST, preferred_element_type=F32)
        return carry

    lax.fori_loop(0, RANK // PANEL, eliminate, 0)
    inverse = []
    for i in range(2):
        pivots = jnp.sum(jnp.where(row == col, gram[i, :, :RANK], 0.0), axis=1, keepdims=True)
        inverse.append(gram[i, :, RANK:] * lax.rsqrt(pivots))

    def solved(values, i):
        return lax.dot_general(
            values, inverse[i], (((1,), (1,)), ((), ())),
            precision=lax.Precision.HIGHEST, preferred_element_type=F32)

    packed_out[:64] = solved(raw_u[...], 0)
    packed_out[64:96] = solved(raw_d[...], 1)

    for copy in tok_sends:
        copy.wait_send()
    drain_first(warm_first + raw_first + raw_two)
    drain_one(plan_a, 0, relay_a)
    drain_one(plan_d, 1, relay_d)
    drain_one(plan_b, 2, relay_b)
    for ring in (warm_ring, raw_ring):
        ring_drain(ring)

    def right_done(route, value):
        packed_out[96 + 64 * route:160 + 64 * route] = solved(value, route) * (1.0 / (nz * ny))

    right_two = scatter_rest(
        1, [(rplan_a, None, rsum_a, rgot_a)], [(rplan_b, rpart_b.at[:, y], rsum_b, rgot_b)],
        rsum_a, rsum_b, rfin_a, rfin_b, right_done)
    drain_first(right_two)
    drain_one(rplan_a, 3, rrelay_a)
    drain_one(rplan_b, 4, rrelay_b)


def unpack(packed, left_u, left_d, right):
    left_u[...] = packed[:64]
    left_d[...] = packed[64:96]
    right[0] = packed[96:160]
    right[1] = packed[160:224]


def on_device(shape, activations, cotangent, gate_pre, up_value, hidden_grad, warm_factors):
    nz, ny, nt = shape
    tokens, width = activations.shape
    rows, ff = gate_pre.shape
    cut_b = 96 - CUT
    half = max(nz, ny) // 2
    packed = pl.pallas_call(
        functools.partial(kernel, nz, ny, nt),
        out_shape=jax.ShapeDtypeStruct((224, RANK), F32),
        in_specs=[pl.BlockSpec(memory_space=pl.ANY)] * 6,
        out_specs=pl.BlockSpec(memory_space=pltpu.VMEM),
        scratch_shapes=[
            pltpu.VMEM((nt, tokens, width), BF16),
            pltpu.VMEM((nt, tokens, width), BF16),
            pltpu.VMEM((rows, ff), BF16),
            pltpu.VMEM((rows, ff), BF16),
            pltpu.VMEM((rows, ff), BF16),
            pltpu.VMEM((2, 1, 64, RANK), F32),
            pltpu.VMEM((2, nz, ny, 64 + FINE, RANK), BF16),
            pltpu.VMEM((rows, 2 * ff), BF16),
            pltpu.VMEM((rows, ff), BF16),
            pltpu.VMEM((nz, ny, CUT, RANK), BF16),
            pltpu.VMEM((nz, ny, 64 - CUT, RANK), BF16),
            pltpu.VMEM((nz, ny, 32, RANK), BF16),
            pltpu.VMEM((nz - 1, ny, CUT, RANK), BF16),
            pltpu.VMEM((ny - 1, nz, 64 - CUT, RANK), BF16),
            pltpu.VMEM((ny - 1, nz, 32, RANK), BF16),
            pltpu.VMEM((ny, CUT, RANK), F32),
            pltpu.VMEM((nz, cut_b, RANK), F32),
            pltpu.VMEM((ny - 1, CUT, RANK), F32),
            pltpu.VMEM((nz - 1, cut_b, RANK), F32),
            pltpu.VMEM((64, RANK), F32),
            pltpu.VMEM((32, RANK), F32),
            pltpu.VMEM((nz, ny, 96, RANK), BF16),
            pltpu.VMEM((nz, ny, 64, RANK), BF16),
            pltpu.VMEM((nz, ny, 64, RANK), BF16),
            pltpu.VMEM((nz - 1, ny, 64, RANK), BF16),
            pltpu.VMEM((ny - 1, nz, 64, RANK), BF16),
            pltpu.VMEM((ny, 64, RANK), F32),
            pltpu.VMEM((nz, 64, RANK), F32),
            pltpu.VMEM((ny - 1, 64, RANK), F32),
            pltpu.VMEM((nz - 1, 64, RANK), F32),
            pltpu.VMEM((2, RANK, 2 * RANK), F32),
            pltpu.VMEM((2, ny // 2, CUT, RANK), BF16),
            pltpu.VMEM((2, nz // 2, 32, RANK), BF16),
            pltpu.VMEM((2, nz // 2, 64 - CUT, RANK), BF16),
            pltpu.VMEM((2, ny // 2, 64, RANK), BF16),
            pltpu.VMEM((2, nz // 2, 64, RANK), BF16),
            pltpu.VMEM((2, ny, CUT, RANK), F32),
            pltpu.VMEM((2, ny, 64, RANK), F32),
            pltpu.SemaphoreType.DMA((6,)),
            pltpu.SemaphoreType.DMA((14,)),
            pltpu.SemaphoreType.DMA((14,)),
            pltpu.SemaphoreType.DMA((2, 2, max(nz, ny) - 1)),
            pltpu.SemaphoreType.DMA((2, 2, max(nz, ny) - 1)),
            pltpu.SemaphoreType.DMA((2, 4, half, 2)),
            pltpu.SemaphoreType.DMA((2, 4, half, 2)),
            pltpu.SemaphoreType.DMA((2, 3, max(nz, ny) - 1)),
            pltpu.SemaphoreType.DMA((2, 3, max(nz, ny) - 1)),
            pltpu.SemaphoreType.DMA((2, 2, max(nz, ny) - 1)),
            pltpu.SemaphoreType.DMA((2, 2, max(nz, ny) - 1)),
            pltpu.SemaphoreType.DMA((5, 2)),
            pltpu.SemaphoreType.DMA((5, 2)),
        ],
        compiler_params=pltpu.CompilerParams(
            collective_id=0, has_side_effects=True, vmem_limit_bytes=56 * 1024 * 1024),
        name="powersgd_step",
    )(activations, cotangent, gate_pre, up_value, hidden_grad, warm_factors)
    left_united, left_down, right = pl.pallas_call(
        unpack,
        out_shape=(
            jax.ShapeDtypeStruct((64, RANK), F32),
            jax.ShapeDtypeStruct((32, RANK), F32),
            jax.ShapeDtypeStruct((2, 64, RANK), F32)),
        name="unpack",
    )(packed)
    return left_united[None], left_down[None], right[:, None]


def solution(mesh):
    dp, nt = mesh.shape["dp"], mesh.shape["tensor"]
    ny = 1 << (dp.bit_length() // 2)
    in_specs = (
        P(("dp", "tensor"), None),
        P(("dp", "tensor"), None),
        P("dp", "tensor"),
        P("dp", "tensor"),
        P("dp", "tensor"),
        P(None, "tensor", "dp", None),
    )
    out_specs = (P("tensor", "dp", None), P("tensor", "dp", None), P(None, "tensor", "dp", None))
    return jax.shard_map(
        functools.partial(on_device, (dp // ny, ny, nt)),
        mesh=mesh, in_specs=in_specs, out_specs=out_specs, check_vma=False)
```

```python
import functools

import jax
import jax.numpy as jnp
from jax import lax
from jax.experimental import pallas as pl
from jax.experimental.pallas import tpu as pltpu
from jax.sharding import PartitionSpec as P

F32 = jnp.float32
BF16 = jnp.bfloat16
RANK = 128
CUT = 48
FINE = 32
PANEL = 16


def tdot(left, right):
    return lax.dot_general(left, right, (((0,), (0,)), ((), ())), preferred_element_type=F32)


def two_halves(values):
    high = values.astype(BF16)
    low = (values - high.astype(F32)).astype(BF16)
    return jnp.concatenate([high, low], axis=1)


def kernel(nz, ny, nt, acts_in, cot_in, gate_in, up_in, hg_in, warm_in,
           packed_out,
           acts, cot, gate, up, hg, warm_f, warm,
           united, hidden,
           part_a, part_b, part_d, got_a, got_b, got_d, sum_a, sum_b, fin_a, fin_b,
           raw_u, raw_d, everyone,
           rpart_a, rpart_b, rgot_a, rgot_b, rsum_a, rsum_b, rfin_a, rfin_b,
           gram, relay_a, relay_d, relay_b, rrelay_a, rrelay_b, keep_a, rkeep_a,
           load_sem, tok_send, tok_recv, first_send, first_recv,
           ring_send, ring_recv, one_send, one_recv, two_send, two_recv, relay_send, relay_recv, hop_send, hop_recv):
    d = lax.axis_index("dp")
    t = lax.axis_index("tensor")
    z, y = d // ny, d % ny
    nx = nt // 2
    x, c = t // 2, t % 2
    tokens = acts_in.shape[0]
    width = acts_in.shape[1]
    ff = gate_in.shape[1]
    tile = ny * 64

    def at_z(p):
        return {"dp": p * ny + y}

    def at_y(p):
        return {"dp": z * ny + p}

    def slot(xx, cc):
        return (xx % nx) * 2 + cc

    def remote(src, dst, send, recv, where):
        return pltpu.make_async_remote_copy(
            src_ref=src, dst_ref=dst, send_sem=send, recv_sem=recv,
            device_id=where, device_id_type=pl.DeviceIdType.MESH)

    loads = [
        pltpu.make_async_copy(src, dst, load_sem.at[i])
        for i, (src, dst) in enumerate([
            (warm_in, warm_f), (gate_in, gate), (up_in, up), (hg_in, hg),
            (acts_in, acts.at[t]), (cot_in, cot.at[t])])
    ]
    for load in loads:
        load.start()

    barrier = pltpu.get_barrier_semaphore()
    to_right = {"tensor": slot(x + 1, c)}
    to_left = {"tensor": slot(x + nx - 1, c)}
    to_twin = {"tensor": slot(x, 1 - c)}

    def greet(where):
        pl.semaphore_signal(barrier, inc=1, device_id=where, device_id_type=pl.DeviceIdType.MESH)

    for where in (to_right, to_left, to_twin):
        greet(where)
    for k in range(1, nz):
        greet(at_z((z + k) % nz))
    for k in range(1, ny):
        greet(at_y((y + k) % ny))
    loads[0].wait()
    coarse = 64 - FINE
    for w in range(2):
        values = warm_f[w, 0]
        high = values.astype(BF16)
        warm[w, z, y, :64] = high
        warm[w, z, y, 64:] = (values - high.astype(F32)).astype(BF16)[coarse:]
    pl.semaphore_wait(barrier, 3 + nz - 1 + ny - 1)

    def exchange(n, me, place, src, dst, send, recv):
        for k in range(1, n):
            to = (me + k) % n
            remote(src(to), dst(k, me), send.at[k - 1], recv.at[k - 1], place(to)).start()

    def landed(n, me, place, src, dst, send, recv, k):
        owner = (me + n - k) % n
        return remote(src(owner), dst(k, owner), send.at[k - 1], recv.at[k - 1], place(owner))

    def first_phase(which, pieces):
        plans = []
        for i, (along_y, block) in enumerate(pieces):
            if along_y:
                plan = (ny, y, at_y, lambda to, b=block: b(z, y), lambda k, o, b=block: b(z, o))
            else:
                plan = (nz, z, at_z, lambda to, b=block: b(z, y), lambda k, o, b=block: b(o, y))
            plans.append(plan + (first_send.at[which, i], first_recv.at[which, i]))
        return plans

    def start_first(plans):
        for plan in plans:
            exchange(*plan)

    def wait_first(plans):
        for plan in plans:
            for k in range(1, plan[0]):
                landed(*plan, k).wait_recv()

    def drain_first(plans):
        for plan in plans:
            for k in range(1, plan[0]):
                landed(*plan, k).wait_send()

    def ring_copy(streams, step, half, i, receiving):
        n, me, place, pieces, turn, which = streams[i]
        if receiving:
            block = (me + n - turn * (1 + step)) % n
        else:
            block = (me + n - turn * step) % n
        to = (me + n + turn) % n
        ref = pieces(block, half)
        return remote(ref, ref, ring_send.at[which, i, step, half],
                      ring_recv.at[which, i, step, half], place(to))

    def ring_moves(n, turn, step):
        if step < n // 2 - 1:
            return (0, 1) if turn > 0 else (1, 0)
        return (0,) if turn > 0 else (1,)

    def ring_start(streams, route):
        for order in range(2):
            for i in (2 * route, 2 * route + 1):
                n, turn = streams[i][0], streams[i][4]
                halves = ring_moves(n, turn, 0)
                if order < len(halves):
                    ring_copy(streams, 0, halves[order], i, False).start()

    def ring_advance(streams, step):
        for order in range(2):
            for i, (n, _, _, _, turn, _) in enumerate(streams):
                if step >= n // 2:
                    continue
                halves = ring_moves(n, turn, step)
                if order < len(halves):
                    half = halves[order]
                    ring_copy(streams, step, half, i, True).wait_recv()
                    if step + 1 < n // 2 and half in ring_moves(n, turn, step + 1):
                        ring_copy(streams, step + 1, half, i, False).start()

    def ring_drain(streams):
        for i, (n, _, _, _, turn, _) in enumerate(streams):
            for step in range(n // 2):
                for half in ring_moves(n, turn, step):
                    ring_copy(streams, step, half, i, False).wait_send()

    def ring_streams(which, z_pieces, y_pieces):
        return [
            (nz, z, at_z, z_pieces, 1, which), (nz, z, at_z, z_pieces, -1, which),
            (ny, y, at_y, y_pieces, 1, which), (ny, y, at_y, y_pieces, -1, which)]

    here = slot(x, c)
    behind, ahead, across = slot(x + nx - 1, c), slot(x + 1, c), slot(x + 2, c)
    twin = [slot(x, 1 - c), slot(x + nx - 1, 1 - c), slot(x + 1, 1 - c), slot(x + 2, 1 - c)]
    tok_sends = []

    def tok(i, src, dst, where):
        copy = remote(src, dst, tok_send.at[i], tok_recv.at[i], where)
        copy.start()
        tok_sends.append(copy)

    def tok_wait(i, ref):
        remote(ref, ref, tok_send.at[i], tok_recv.at[i], to_twin).wait_recv()

    warm_first = first_phase(0, [
        (True, lambda zz, yy: warm.at[0, zz, yy]), (False, lambda zz, yy: warm.at[1, zz, yy])])
    start_first(warm_first)
    tok(0, acts_in, acts.at[here], to_right)
    tok(3, cot_in, cot.at[here], to_left)
    tok(1, cot_in, cot.at[here], to_right)
    tok(2, acts_in, acts.at[here], to_left)
    tok(6, acts_in, acts.at[here], to_twin)
    tok(10, cot_in, cot.at[here], to_twin)

    for load in loads[1:4]:
        load.wait()

    def backward(i, carry):
        rows = pl.ds(pl.multiple_of(i * 16, 16), 16)
        gate_w = gate[rows, :].astype(F32)
        up_w = up[rows, :].astype(F32)
        hg_w = hg[rows, :].astype(F32)
        sigma = jax.nn.sigmoid(gate_w)
        active = gate_w * sigma
        hidden[rows, :] = (active * up_w).astype(BF16)
        united[rows, :ff] = (hg_w * up_w * sigma * (1.0 + gate_w * (1.0 - sigma))).astype(BF16)
        united[rows, ff:] = (hg_w * active).astype(BF16)
        return carry

    steps = gate_in.shape[0] // 16
    lax.fori_loop(0, steps // 2, backward, 0)

    halves_y, halves_z = ny // 2, nz // 2
    warm_ring = ring_streams(
        0,
        lambda b, h: warm.at[0, b, pl.ds(h * halves_y, halves_y)],
        lambda b, h: warm.at[1, pl.ds(h * halves_z, halves_z), b])
    for route in range(2):
        wait_first(warm_first[route:route + 1])
        ring_start(warm_ring, route)
    lax.fori_loop(steps // 2, steps, backward, 0)

    tok_wait(0, acts.at[behind])
    tok(4, acts.at[behind], acts.at[behind], to_right)
    tok(7, acts.at[behind], acts.at[behind], to_twin)
    tok_wait(3, cot.at[ahead])
    tok(5, cot.at[ahead], cot.at[ahead], to_left)
    tok(12, cot.at[ahead], cot.at[ahead], to_twin)
    ring_advance(warm_ring, 0)
    tok_wait(2, acts.at[ahead])
    tok(8, acts.at[ahead], acts.at[ahead], to_twin)
    tok_wait(1, cot.at[behind])
    tok(11, cot.at[behind], cot.at[behind], to_twin)
    for step in range(1, max(nz, ny) // 2):
        ring_advance(warm_ring, step)
    tok_wait(4, acts.at[across])
    tok(9, acts.at[across], acts.at[across], to_twin)
    tok_wait(5, cot.at[across])
    tok(13, cot.at[across], cot.at[across], to_twin)
    for load in loads[4:]:
        load.wait()
    for i in range(4):
        tok_wait(6 + i, acts.at[twin[i]])
        tok_wait(10 + i, cot.at[twin[i]])

    group = nz // 2
    no_fine = jnp.zeros((group, ny, coarse, RANK), BF16)

    def probe(tokens_ref, w):
        pair = jnp.zeros((nt * tokens, 2 * RANK), F32)
        for i in range(nz // group):
            span = group * tile
            rows = tokens_ref[:, :, i * span:(i + 1) * span].reshape(nt * tokens, span)
            blocks = warm[w, i * group:(i + 1) * group]
            factor = jnp.concatenate(
                [blocks[:, :, :64].reshape(span, RANK),
                 jnp.concatenate([no_fine, blocks[:, :, 64:]], axis=2).reshape(span, RANK)], axis=1)
            pair = pair + jnp.dot(rows, factor, preferred_element_type=F32)
        return two_halves(pair[:, :RANK] + pair[:, RANK:])

    def folded(pair):
        return pair[:, :RANK] + pair[:, RANK:]

    def along_z(i, j, a, ga):
        return (nz, z, at_z, lambda to: a.at[to], lambda k, o: ga.at[k - 1],
                one_send.at[i, j], one_recv.at[i, j])

    def along_y(i, j, b, gb):
        return (ny, y, at_y, lambda to: b.at[:, to], lambda k, o: gb.at[k - 1],
                one_send.at[i, j], one_recv.at[i, j])

    def send_one(plan, k):
        n, me, place, src, dst, send, recv = plan
        to = (me + k) % n
        remote(src(to), dst(k, me), send.at[k - 1], recv.at[k - 1], place(to)).start()

    def near(n):
        return [k for k in range(1, n) if abs(k - n // 2) > 1]

    def arriving(n):
        return [k for k in range(1, n) if k != n // 2]

    def is_near(k, n):
        return (k != 0) & (k != n // 2) & (k != n // 2 - 1) & (k != n // 2 + 1)

    def in_order(j, n):
        j = (j + n - 1) % n
        m, odd = (j + 1) // 2, j % 2
        return (odd * m + (1 - odd) * (n - m)) % n

    def relay_copies(plan, r, relay):
        n, me, place, src = plan[:4]
        block = src((me + n // 2) % n)
        size = relay.shape[1]
        return [
            remote(block.at[pl.ds(h * size, size)], relay.at[h], relay_send.at[r, h],
                   relay_recv.at[r, h], place((me + (1, n - 1)[h]) % n)) for h in range(2)]

    def far_out(plan, r, relay):
        for copy in relay_copies(plan, r, relay):
            copy.start()

    def near_out(plan):
        for k in near(plan[0]):
            send_one(plan, k)

    def relayed(plan, r, relay, keep):
        n, me, place, src = plan[:4]
        size = relay.shape[1]
        for h, copy in enumerate(relay_copies(plan, r, relay)):
            copy.wait_recv()
            k = n // 2 - 1 + 2 * h
            piece = src((me + k) % n).at[pl.ds(h * size, size)]
            own = piece if keep is None else keep.at[h, pl.ds(h * size, size)]
            piece[...] = (own[...].astype(F32) + relay[h].astype(F32)).astype(BF16)
            send_one(plan, k)

    def drain_one(plan, r, relay):
        for copy in relay_copies(plan, r, relay):
            copy.wait_send()
        for k in arriving(plan[0]):
            landed(*plan, k).wait_send()

    plan_a = along_z(0, 0, part_a, got_a)
    plan_d = along_y(0, 1, part_d, got_d)
    plan_b = along_y(0, 2, part_b, got_b)

    probe_d = probe(cot, 1)

    def down_tile(i, carry):
        columns = pl.ds(pl.multiple_of(i * tile, tile), tile)
        block = folded(tdot(hidden[:, columns], probe_d)).reshape(2, ny, 32, RANK)
        part_d[pl.ds(2 * i, 2)] = block.astype(BF16)
        return carry

    lax.fori_loop(0, ff // tile, down_tile, 0)
    far_out(plan_d, 1, relay_d)
    near_out(plan_d)

    probe_u = probe(acts, 0)

    def row_out(j, plan, r, relay, keep, total, store, compute):
        k = in_order(j, nz)
        i = (z + k) % nz
        block = folded(compute(pl.ds(pl.multiple_of(i * tile, tile), tile))).reshape(ny, 64, RANK)
        store(i, block.astype(BF16))
        rows = total.shape[1]

        @pl.when(k == 0)
        def _():
            total[...] = block[:, :rows]

        for h in range(2):
            @pl.when(k == nz // 2 - 1 + 2 * h)
            def _():
                keep[h] = block[:, :rows]

        @pl.when(k == nz // 2)
        def _():
            far_out(plan, r, relay)

        @pl.when(is_near(k, nz))
        def _():
            send_one(plan, k)

    def store_raw(i, block):
        part_a[i] = block[:, :CUT]
        part_b[i] = block[:, CUT:]

    def united_tile(j, carry):
        row_out(j, plan_a, 0, relay_a, keep_a, sum_a, store_raw,
                lambda columns: tdot(united[:, columns], probe_u))
        return carry

    lax.fori_loop(0, nz, united_tile, 0)
    far_out(plan_b, 2, relay_b)
    relayed(plan_a, 0, relay_a, keep_a)
    near_out(plan_b)
    relayed(plan_d, 1, relay_d, None)
    relayed(plan_b, 2, relay_b, None)

    def scatter_rest(i, firsts_a, firsts_b, sa, sb, fa, fb, done):
        two = [
            (ny, y, at_y, lambda to: sa.at[to], lambda k, o: fa.at[k - 1], two_send.at[i, 0], two_recv.at[i, 0]),
            (nz, z, at_z, lambda to: sb.at[to], lambda k, o: fb.at[k - 1], two_send.at[i, 1], two_recv.at[i, 1])]
        for firsts, second in ((firsts_a, two[0]), (firsts_b, two[1])):
            for plan, own, total, got in firsts:
                if own is not None:
                    total[...] = own[...].astype(F32)
                for k in arriving(plan[0]):
                    landed(*plan, k).wait_recv()
                    total[...] += got[k - 1].astype(F32)
            exchange(*second)
        for route, (plan, total, fin, me) in enumerate(((two[0], sa, fa, y), (two[1], sb, fb, z))):
            value = total[me]
            for k in range(1, plan[0]):
                landed(*plan, k).wait_recv()
                value = value + fin[k - 1]
            done(route, value)
        return two

    raw_first = first_phase(1, [
        (True, lambda zz, yy: everyone.at[zz, yy, pl.ds(0, CUT)]),
        (False, lambda zz, yy: everyone.at[zz, yy, pl.ds(CUT, 96 - CUT)])])

    def raw_done(route, value):
        if route == 0:
            raw_u[:CUT] = value
            everyone[z, y, :CUT] = value.astype(BF16)
        else:
            raw_u[CUT:] = value[:64 - CUT]
            raw_d[...] = value[64 - CUT:]
            everyone[z, y, CUT:] = value.astype(BF16)
        start_first(raw_first[route:route + 1])

    raw_two = scatter_rest(
        0, [(plan_a, None, sum_a, got_a)],
        [(plan_d, part_d.at[:, y], sum_b.at[:, pl.ds(64 - CUT, 32)], got_d),
         (plan_b, part_b.at[:, y], sum_b.at[:, pl.ds(0, 64 - CUT)], got_b)],
        sum_a, sum_b, fin_a, fin_b, raw_done)

    def hops(route):
        n, me, place = ((nz, z, at_z), (ny, y, at_y))[route]

        def block(offset, half=None):
            b = (me + n + offset) % n
            if route == 0:
                part = slice(None) if half is None else pl.ds(half * halves_y, halves_y)
                return everyone.at[b, part, pl.ds(0, CUT)]
            part = slice(None) if half is None else pl.ds(half * halves_z, halves_z)
            return everyone.at[part, b, pl.ds(CUT, 96 - CUT)]

        def copy(i, ref, offset):
            return remote(ref, ref, hop_send.at[route, i], hop_recv.at[route, i],
                          place((me + n + offset) % n))

        sent = [copy(0, block(0), 2), copy(1, block(0), -2), copy(2, block(0), 1), copy(3, block(0), -1),
                copy(4, block(-2), 1), copy(5, block(2), -1), copy(6, block(-2, 0), 2), copy(7, block(2, 1), -2)]
        came = [copy(0, block(-2), 2), copy(1, block(2), -2), copy(2, block(-1), 1), copy(3, block(1), -1),
                copy(4, block(-3), 1), copy(5, block(3), -1), copy(6, block(-4, 0), 2), copy(7, block(4, 1), -2)]
        return sent, came

    raw_hops = [hops(0), hops(1)]
    for route in range(2):
        wait_first(raw_first[route:route + 1])
        for copy in raw_hops[route][0][:4]:
            copy.start()
    for side in range(2):
        for sent, came in raw_hops:
            came[side].wait_recv()
            sent[4 + side].start()
            sent[6 + side].start()
    for sent, came in raw_hops:
        for copy in came[2:]:
            copy.wait_recv()

    flat_u = everyone[:, :, :64].reshape(2 * ff, RANK)
    mixed_u = two_halves(jnp.dot(united[...], flat_u, preferred_element_type=F32))
    flat_d = everyone[:, :, 64:].reshape(ff, RANK)
    mixed_d = two_halves(jnp.dot(hidden[...], flat_d, preferred_element_type=F32))
    rplan_a = along_z(1, 0, rpart_a, rgot_a)
    rplan_b = along_y(1, 1, rpart_b, rgot_b)
    rounds = ny // 2
    per_round = nz // rounds

    def store_right(i, block):
        rpart_a[i] = block

    def right_round(q, carry):
        for extra in range(per_round):
            row_out(q * per_round + extra, rplan_a, 3, rrelay_a, rkeep_a, rsum_a, store_right,
                    lambda columns: tdot(acts[:, :, columns].reshape(nt * tokens, tile), mixed_u))

        pair = (y // 2 + q + rounds // 2) % rounds
        rows = jnp.concatenate(
            [cot[:, :, pl.ds(pl.multiple_of(i * tile + pair * 128, 128), 128)].reshape(
                nt * tokens, 128) for i in range(nz)], axis=1)
        rpart_b[:, pl.ds(2 * pair, 2)] = folded(
            tdot(rows, mixed_d)).reshape(nz, 2, 64, RANK).astype(BF16)
        for extra in range(2):
            k = (2 * pair + extra + ny - y) % ny

            @pl.when(k == ny // 2)
            def _():
                far_out(rplan_b, 4, rrelay_b)

            @pl.when(is_near(k, ny))
            def _():
                send_one(rplan_b, k)
        return carry

    lax.fori_loop(0, rounds, right_round, 0)
    relayed(rplan_a, 3, rrelay_a, rkeep_a)
    relayed(rplan_b, 4, rrelay_b, None)

    row = lax.broadcasted_iota(jnp.int32, (RANK, RANK), 0)
    col = lax.broadcasted_iota(jnp.int32, (RANK, RANK), 1)
    for i, flat in enumerate((flat_u, flat_d)):
        gram[i, :, :RANK] = tdot(flat, flat)
        gram[i, :, RANK:] = (row == col).astype(F32)
    lane = lax.broadcasted_iota(jnp.int32, (PANEL, RANK), 1)
    sub = lax.broadcasted_iota(jnp.int32, (PANEL, RANK), 0)
    sub_one = lax.broadcasted_iota(jnp.int32, (PANEL, 1), 0)

    def eliminate(b, carry):
        base = pl.multiple_of(b * PANEL, PANEL)
        rows = pl.ds(base, PANEL)
        panels = [gram[i, rows, :] for i in range(2)]
        for j in range(PANEL):
            for i in range(2):
                panel = panels[i]
                column = jnp.sum(
                    jnp.where(lane == base + j, panel[:, :RANK], 0.0), axis=1, keepdims=True)
                factor = jnp.where(sub_one > j, column / column[j:j + 1], 0.0)
                panels[i] = panel - factor * panel[j:j + 1]
        for i in range(2):
            panel = panels[i]
            gram[i, rows, :] = panel
            head = panel[:, :RANK]
            pivots = jnp.sum(jnp.where(lane == base + sub, head, 0.0), axis=1, keepdims=True)
            weights = jnp.where(lane >= base + PANEL, head / pivots, 0.0)
            gram[i] -= lax.dot_general(
                weights, panel, (((0,), (0,)), ((), ())),
                precision=lax.Precision.HIGHEST, preferred_element_type=F32)
        return carry

    lax.fori_loop(0, RANK // PANEL, eliminate, 0)
    inverse = []
    for i in range(2):
        pivots = jnp.sum(jnp.where(row == col, gram[i, :, :RANK], 0.0), axis=1, keepdims=True)
        inverse.append(gram[i, :, RANK:] * lax.rsqrt(pivots))

    def solved(values, i):
        return lax.dot_general(
            values, inverse[i], (((1,), (1,)), ((), ())),
            precision=lax.Precision.HIGHEST, preferred_element_type=F32)

    packed_out[:64] = solved(raw_u[...], 0)
    packed_out[64:96] = solved(raw_d[...], 1)

    for copy in tok_sends:
        copy.wait_send()
    drain_first(warm_first + raw_first + raw_two)
    drain_one(plan_a, 0, relay_a)
    drain_one(plan_d, 1, relay_d)
    drain_one(plan_b, 2, relay_b)
    ring_drain(warm_ring)
    for sent, came in raw_hops:
        for copy in sent:
            copy.wait_send()

    def right_done(route, value):
        packed_out[96 + 64 * route:160 + 64 * route] = solved(value, route) * (1.0 / (nz * ny))

    right_two = scatter_rest(
        1, [(rplan_a, None, rsum_a, rgot_a)], [(rplan_b, rpart_b.at[:, y], rsum_b, rgot_b)],
        rsum_a, rsum_b, rfin_a, rfin_b, right_done)
    drain_first(right_two)
    drain_one(rplan_a, 3, rrelay_a)
    drain_one(rplan_b, 4, rrelay_b)


def unpack(packed, left_u, left_d, right):
    left_u[...] = packed[:64]
    left_d[...] = packed[64:96]
    right[0] = packed[96:160]
    right[1] = packed[160:224]


def on_device(shape, activations, cotangent, gate_pre, up_value, hidden_grad, warm_factors):
    nz, ny, nt = shape
    tokens, width = activations.shape
    rows, ff = gate_pre.shape
    cut_b = 96 - CUT
    half = max(nz, ny) // 2
    packed = pl.pallas_call(
        functools.partial(kernel, nz, ny, nt),
        out_shape=jax.ShapeDtypeStruct((224, RANK), F32),
        in_specs=[pl.BlockSpec(memory_space=pl.ANY)] * 6,
        out_specs=pl.BlockSpec(memory_space=pltpu.VMEM),
        scratch_shapes=[
            pltpu.VMEM((nt, tokens, width), BF16),
            pltpu.VMEM((nt, tokens, width), BF16),
            pltpu.VMEM((rows, ff), BF16),
            pltpu.VMEM((rows, ff), BF16),
            pltpu.VMEM((rows, ff), BF16),
            pltpu.VMEM((2, 1, 64, RANK), F32),
            pltpu.VMEM((2, nz, ny, 64 + FINE, RANK), BF16),
            pltpu.VMEM((rows, 2 * ff), BF16),
            pltpu.VMEM((rows, ff), BF16),
            pltpu.VMEM((nz, ny, CUT, RANK), BF16),
            pltpu.VMEM((nz, ny, 64 - CUT, RANK), BF16),
            pltpu.VMEM((nz, ny, 32, RANK), BF16),
            pltpu.VMEM((nz - 1, ny, CUT, RANK), BF16),
            pltpu.VMEM((ny - 1, nz, 64 - CUT, RANK), BF16),
            pltpu.VMEM((ny - 1, nz, 32, RANK), BF16),
            pltpu.VMEM((ny, CUT, RANK), F32),
            pltpu.VMEM((nz, cut_b, RANK), F32),
            pltpu.VMEM((ny - 1, CUT, RANK), F32),
            pltpu.VMEM((nz - 1, cut_b, RANK), F32),
            pltpu.VMEM((64, RANK), F32),
            pltpu.VMEM((32, RANK), F32),
            pltpu.VMEM((nz, ny, 96, RANK), BF16),
            pltpu.VMEM((nz, ny, 64, RANK), BF16),
            pltpu.VMEM((nz, ny, 64, RANK), BF16),
            pltpu.VMEM((nz - 1, ny, 64, RANK), BF16),
            pltpu.VMEM((ny - 1, nz, 64, RANK), BF16),
            pltpu.VMEM((ny, 64, RANK), F32),
            pltpu.VMEM((nz, 64, RANK), F32),
            pltpu.VMEM((ny - 1, 64, RANK), F32),
            pltpu.VMEM((nz - 1, 64, RANK), F32),
            pltpu.VMEM((2, RANK, 2 * RANK), F32),
            pltpu.VMEM((2, ny // 2, CUT, RANK), BF16),
            pltpu.VMEM((2, nz // 2, 32, RANK), BF16),
            pltpu.VMEM((2, nz // 2, 64 - CUT, RANK), BF16),
            pltpu.VMEM((2, ny // 2, 64, RANK), BF16),
            pltpu.VMEM((2, nz // 2, 64, RANK), BF16),
            pltpu.VMEM((2, ny, CUT, RANK), F32),
            pltpu.VMEM((2, ny, 64, RANK), F32),
            pltpu.SemaphoreType.DMA((6,)),
            pltpu.SemaphoreType.DMA((14,)),
            pltpu.SemaphoreType.DMA((14,)),
            pltpu.SemaphoreType.DMA((2, 2, max(nz, ny) - 1)),
            pltpu.SemaphoreType.DMA((2, 2, max(nz, ny) - 1)),
            pltpu.SemaphoreType.DMA((2, 4, half, 2)),
            pltpu.SemaphoreType.DMA((2, 4, half, 2)),
            pltpu.SemaphoreType.DMA((2, 3, max(nz, ny) - 1)),
            pltpu.SemaphoreType.DMA((2, 3, max(nz, ny) - 1)),
            pltpu.SemaphoreType.DMA((2, 2, max(nz, ny) - 1)),
            pltpu.SemaphoreType.DMA((2, 2, max(nz, ny) - 1)),
            pltpu.SemaphoreType.DMA((5, 2)),
            pltpu.SemaphoreType.DMA((5, 2)),
            pltpu.SemaphoreType.DMA((2, 8)),
            pltpu.SemaphoreType.DMA((2, 8)),
        ],
        compiler_params=pltpu.CompilerParams(
            collective_id=0, has_side_effects=True, vmem_limit_bytes=56 * 1024 * 1024),
        name="powersgd_step",
    )(activations, cotangent, gate_pre, up_value, hidden_grad, warm_factors)
    left_united, left_down, right = pl.pallas_call(
        unpack,
        out_shape=(
            jax.ShapeDtypeStruct((64, RANK), F32),
            jax.ShapeDtypeStruct((32, RANK), F32),
            jax.ShapeDtypeStruct((2, 64, RANK), F32)),
        name="unpack",
    )(packed)
    return left_united[None], left_down[None], right[:, None]


def solution(mesh):
    dp, nt = mesh.shape["dp"], mesh.shape["tensor"]
    ny = 1 << (dp.bit_length() // 2)
    in_specs = (
        P(("dp", "tensor"), None),
        P(("dp", "tensor"), None),
        P("dp", "tensor"),
        P("dp", "tensor"),
        P("dp", "tensor"),
        P(None, "tensor", "dp", None),
    )
    out_specs = (P("tensor", "dp", None), P("tensor", "dp", None), P(None, "tensor", "dp", None))
    return jax.shard_map(
        functools.partial(on_device, (dp // ny, ny, nt)),
        mesh=mesh, in_specs=in_specs, out_specs=out_specs, check_vma=False)
```

```python
import functools

import jax
import jax.numpy as jnp
from jax import lax
from jax.experimental import pallas as pl
from jax.experimental.pallas import tpu as pltpu
from jax.sharding import PartitionSpec as P

F32 = jnp.float32
BF16 = jnp.bfloat16
RANK = 128
CUT = 48
FINE = 32
PANEL = 16


def tdot(left, right):
    return lax.dot_general(left, right, (((0,), (0,)), ((), ())), preferred_element_type=F32)


def two_halves(values):
    high = values.astype(BF16)
    low = (values - high.astype(F32)).astype(BF16)
    return jnp.concatenate([high, low], axis=1)


def kernel(nz, ny, nt, acts_in, cot_in, gate_in, up_in, hg_in, warm_in,
           packed_out,
           acts, cot, gate, up, hg, warm_f, warm,
           united, hidden,
           part_a, part_b, part_d, got_a, got_b, got_d, sum_a, sum_b, fin_a, fin_b,
           raw_u, raw_d, everyone,
           rpart_a, rpart_b, rgot_a, rgot_b, rsum_a, rsum_b, rfin_a, rfin_b,
           gram, relay_a, relay_d, relay_b, rrelay_a, rrelay_b, keep_a, rkeep_a,
           load_sem, tok_send, tok_recv, first_send, first_recv,
           ring_send, ring_recv, one_send, one_recv, two_send, two_recv, relay_send, relay_recv, hop_send, hop_recv):
    d = lax.axis_index("dp")
    t = lax.axis_index("tensor")
    z, y = d // ny, d % ny
    nx = nt // 2
    x, c = t // 2, t % 2
    tokens = acts_in.shape[0]
    width = acts_in.shape[1]
    ff = gate_in.shape[1]
    tile = ny * 64

    def at_z(p):
        return {"dp": p * ny + y}

    def at_y(p):
        return {"dp": z * ny + p}

    def slot(xx, cc):
        return (xx % nx) * 2 + cc

    def remote(src, dst, send, recv, where):
        return pltpu.make_async_remote_copy(
            src_ref=src, dst_ref=dst, send_sem=send, recv_sem=recv,
            device_id=where, device_id_type=pl.DeviceIdType.MESH)

    loads = [
        pltpu.make_async_copy(src, dst, load_sem.at[i])
        for i, (src, dst) in enumerate([
            (warm_in, warm_f), (gate_in, gate), (up_in, up), (hg_in, hg),
            (acts_in, acts.at[t]), (cot_in, cot.at[t])])
    ]
    for load in loads:
        load.start()

    barrier = pltpu.get_barrier_semaphore()
    to_right = {"tensor": slot(x + 1, c)}
    to_left = {"tensor": slot(x + nx - 1, c)}
    to_twin = {"tensor": slot(x, 1 - c)}

    def greet(where):
        pl.semaphore_signal(barrier, inc=1, device_id=where, device_id_type=pl.DeviceIdType.MESH)

    for where in (to_right, to_left, to_twin):
        greet(where)
    for k in range(1, nz):
        greet(at_z((z + k) % nz))
    for k in range(1, ny):
        greet(at_y((y + k) % ny))
    loads[0].wait()
    coarse = 64 - FINE
    for w in range(2):
        values = warm_f[w, 0]
        high = values.astype(BF16)
        warm[w, z, y, :64] = high
        warm[w, z, y, 64:] = (values - high.astype(F32)).astype(BF16)[coarse:]
    pl.semaphore_wait(barrier, 3 + nz - 1 + ny - 1)

    def exchange(n, me, place, src, dst, send, recv):
        for k in range(1, n):
            to = (me + k) % n
            remote(src(to), dst(k, me), send.at[k - 1], recv.at[k - 1], place(to)).start()

    def landed(n, me, place, src, dst, send, recv, k):
        owner = (me + n - k) % n
        return remote(src(owner), dst(k, owner), send.at[k - 1], recv.at[k - 1], place(owner))

    def first_phase(which, pieces):
        plans = []
        for i, (along_y, block) in enumerate(pieces):
            if along_y:
                plan = (ny, y, at_y, lambda to, b=block: b(z, y), lambda k, o, b=block: b(z, o))
            else:
                plan = (nz, z, at_z, lambda to, b=block: b(z, y), lambda k, o, b=block: b(o, y))
            plans.append(plan + (first_send.at[which, i], first_recv.at[which, i]))
        return plans

    def start_first(plans):
        for plan in plans:
            exchange(*plan)

    def wait_first(plans):
        for plan in plans:
            for k in range(1, plan[0]):
                landed(*plan, k).wait_recv()

    def drain_first(plans):
        for plan in plans:
            for k in range(1, plan[0]):
                landed(*plan, k).wait_send()

    def ring_copy(streams, step, half, i, receiving):
        n, me, place, pieces, turn, which = streams[i]
        if receiving:
            block = (me + n - turn * (1 + step)) % n
        else:
            block = (me + n - turn * step) % n
        to = (me + n + turn) % n
        ref = pieces(block, half)
        return remote(ref, ref, ring_send.at[which, i, step, half],
                      ring_recv.at[which, i, step, half], place(to))

    def ring_moves(n, turn, step):
        if step < n // 2 - 1:
            return (0, 1) if turn > 0 else (1, 0)
        return (0,) if turn > 0 else (1,)

    def ring_start(streams, route):
        for order in range(2):
            for i in (2 * route, 2 * route + 1):
                n, turn = streams[i][0], streams[i][4]
                halves = ring_moves(n, turn, 0)
                if order < len(halves):
                    ring_copy(streams, 0, halves[order], i, False).start()

    def ring_advance(streams, step):
        for order in range(2):
            for i, (n, _, _, _, turn, _) in enumerate(streams):
                if step >= n // 2:
                    continue
                halves = ring_moves(n, turn, step)
                if order < len(halves):
                    half = halves[order]
                    ring_copy(streams, step, half, i, True).wait_recv()
                    if step + 1 < n // 2 and half in ring_moves(n, turn, step + 1):
                        ring_copy(streams, step + 1, half, i, False).start()

    def ring_drain(streams):
        for i, (n, _, _, _, turn, _) in enumerate(streams):
            for step in range(n // 2):
                for half in ring_moves(n, turn, step):
                    ring_copy(streams, step, half, i, False).wait_send()

    def ring_streams(which, z_pieces, y_pieces):
        return [
            (nz, z, at_z, z_pieces, 1, which), (nz, z, at_z, z_pieces, -1, which),
            (ny, y, at_y, y_pieces, 1, which), (ny, y, at_y, y_pieces, -1, which)]

    here = slot(x, c)
    behind, ahead, across = slot(x + nx - 1, c), slot(x + 1, c), slot(x + 2, c)
    twin = [slot(x, 1 - c), slot(x + nx - 1, 1 - c), slot(x + 1, 1 - c), slot(x + 2, 1 - c)]
    tok_sends = []

    def tok(i, src, dst, where):
        copy = remote(src, dst, tok_send.at[i], tok_recv.at[i], where)
        copy.start()
        tok_sends.append(copy)

    def tok_wait(i, ref):
        remote(ref, ref, tok_send.at[i], tok_recv.at[i], to_twin).wait_recv()

    warm_first = first_phase(0, [
        (True, lambda zz, yy: warm.at[0, zz, yy]), (False, lambda zz, yy: warm.at[1, zz, yy])])
    start_first(warm_first)
    tok(0, acts_in, acts.at[here], to_right)
    tok(3, cot_in, cot.at[here], to_left)
    tok(1, cot_in, cot.at[here], to_right)
    tok(2, acts_in, acts.at[here], to_left)
    tok(6, acts_in, acts.at[here], to_twin)
    tok(10, cot_in, cot.at[here], to_twin)

    for load in loads[1:4]:
        load.wait()

    def backward(i, carry):
        rows = pl.ds(pl.multiple_of(i * 16, 16), 16)
        gate_w = gate[rows, :].astype(F32)
        up_w = up[rows, :].astype(F32)
        hg_w = hg[rows, :].astype(F32)
        sigma = jax.nn.sigmoid(gate_w)
        active = gate_w * sigma
        hidden[rows, :] = (active * up_w).astype(BF16)
        united[rows, :ff] = (hg_w * up_w * sigma * (1.0 + gate_w * (1.0 - sigma))).astype(BF16)
        united[rows, ff:] = (hg_w * active).astype(BF16)
        return carry

    steps = gate_in.shape[0] // 16
    lax.fori_loop(0, steps // 2, backward, 0)

    halves_y, halves_z = ny // 2, nz // 2
    warm_ring = ring_streams(
        0,
        lambda b, h: warm.at[0, b, pl.ds(h * halves_y, halves_y)],
        lambda b, h: warm.at[1, pl.ds(h * halves_z, halves_z), b])
    for route in range(2):
        wait_first(warm_first[route:route + 1])
        ring_start(warm_ring, route)
    lax.fori_loop(steps // 2, steps, backward, 0)

    tok_wait(0, acts.at[behind])
    tok(4, acts.at[behind], acts.at[behind], to_right)
    tok(7, acts.at[behind], acts.at[behind], to_twin)
    tok_wait(3, cot.at[ahead])
    tok(5, cot.at[ahead], cot.at[ahead], to_left)
    tok(12, cot.at[ahead], cot.at[ahead], to_twin)
    ring_advance(warm_ring, 0)
    tok_wait(2, acts.at[ahead])
    tok(8, acts.at[ahead], acts.at[ahead], to_twin)
    tok_wait(1, cot.at[behind])
    tok(11, cot.at[behind], cot.at[behind], to_twin)
    ring_advance(warm_ring, 1)
    tok_wait(4, acts.at[across])
    tok(9, acts.at[across], acts.at[across], to_twin)
    tok_wait(5, cot.at[across])
    tok(13, cot.at[across], cot.at[across], to_twin)
    for step in range(2, max(nz, ny) // 2):
        ring_advance(warm_ring, step)
    for load in loads[4:]:
        load.wait()
    for i in range(4):
        tok_wait(10 + i, cot.at[twin[i]])

    group = nz // 2
    no_fine = jnp.zeros((group, ny, coarse, RANK), BF16)

    def probe(tokens_ref, w):
        pair = jnp.zeros((nt * tokens, 2 * RANK), F32)
        for i in range(nz // group):
            span = group * tile
            rows = tokens_ref[:, :, i * span:(i + 1) * span].reshape(nt * tokens, span)
            blocks = warm[w, i * group:(i + 1) * group]
            factor = jnp.concatenate(
                [blocks[:, :, :64].reshape(span, RANK),
                 jnp.concatenate([no_fine, blocks[:, :, 64:]], axis=2).reshape(span, RANK)], axis=1)
            pair = pair + jnp.dot(rows, factor, preferred_element_type=F32)
        return two_halves(pair[:, :RANK] + pair[:, RANK:])

    def folded(pair):
        return pair[:, :RANK] + pair[:, RANK:]

    def along_z(i, j, a, ga):
        return (nz, z, at_z, lambda to: a.at[to], lambda k, o: ga.at[k - 1],
                one_send.at[i, j], one_recv.at[i, j])

    def along_y(i, j, b, gb):
        return (ny, y, at_y, lambda to: b.at[:, to], lambda k, o: gb.at[k - 1],
                one_send.at[i, j], one_recv.at[i, j])

    def send_one(plan, k):
        n, me, place, src, dst, send, recv = plan
        to = (me + k) % n
        remote(src(to), dst(k, me), send.at[k - 1], recv.at[k - 1], place(to)).start()

    def near(n):
        return [k for k in range(1, n) if abs(k - n // 2) > 1]

    def arriving(n):
        return [k for k in range(1, n) if k != n // 2]

    def is_near(k, n):
        return (k != 0) & (k != n // 2) & (k != n // 2 - 1) & (k != n // 2 + 1)

    def in_order(j, n):
        j = (j + n - 1) % n
        m, odd = (j + 1) // 2, j % 2
        return (odd * m + (1 - odd) * (n - m)) % n

    def relay_copies(plan, r, relay):
        n, me, place, src = plan[:4]
        block = src((me + n // 2) % n)
        size = relay.shape[1]
        return [
            remote(block.at[pl.ds(h * size, size)], relay.at[h], relay_send.at[r, h],
                   relay_recv.at[r, h], place((me + (1, n - 1)[h]) % n)) for h in range(2)]

    def far_out(plan, r, relay):
        for copy in relay_copies(plan, r, relay):
            copy.start()

    def near_out(plan):
        for k in near(plan[0]):
            send_one(plan, k)

    def relayed(plan, r, relay, keep):
        n, me, place, src = plan[:4]
        size = relay.shape[1]
        for h, copy in enumerate(relay_copies(plan, r, relay)):
            copy.wait_recv()
            k = n // 2 - 1 + 2 * h
            piece = src((me + k) % n).at[pl.ds(h * size, size)]
            own = piece if keep is None else keep.at[h, pl.ds(h * size, size)]
            piece[...] = (own[...].astype(F32) + relay[h].astype(F32)).astype(BF16)
            send_one(plan, k)

    def drain_one(plan, r, relay):
        for copy in relay_copies(plan, r, relay):
            copy.wait_send()
        for k in arriving(plan[0]):
            landed(*plan, k).wait_send()

    plan_a = along_z(0, 0, part_a, got_a)
    plan_d = along_y(0, 1, part_d, got_d)
    plan_b = along_y(0, 2, part_b, got_b)

    probe_d = probe(cot, 1)

    for i in range(2):
        block = folded(tdot(hidden[:, i * ff // 2:(i + 1) * ff // 2], probe_d))
        part_d[i * nz // 2:(i + 1) * nz // 2] = block.reshape(nz // 2, ny, 32, RANK).astype(BF16)
    far_out(plan_d, 1, relay_d)
    near_out(plan_d)

    for i in range(4):
        tok_wait(6 + i, acts.at[twin[i]])
    probe_u = probe(acts, 0)

    def row_out(j, plan, r, relay, keep, total, store, compute):
        k = in_order(j, nz)
        i = (z + k) % nz
        block = folded(compute(pl.ds(pl.multiple_of(i * tile, tile), tile))).reshape(ny, 64, RANK)
        store(i, block.astype(BF16))
        rows = total.shape[1]

        @pl.when(k == 0)
        def _():
            total[...] = block[:, :rows]

        for h in range(2):
            @pl.when(k == nz // 2 - 1 + 2 * h)
            def _():
                keep[h] = block[:, :rows]

        @pl.when(k == nz // 2)
        def _():
            far_out(plan, r, relay)

        @pl.when(is_near(k, nz))
        def _():
            send_one(plan, k)

    def store_raw(i, block):
        part_a[i] = block[:, :CUT]
        part_b[i] = block[:, CUT:]

    def united_tile(j, carry):
        row_out(j, plan_a, 0, relay_a, keep_a, sum_a, store_raw,
                lambda columns: tdot(united[:, columns], probe_u))
        return carry

    lax.fori_loop(0, nz, united_tile, 0)
    far_out(plan_b, 2, relay_b)
    relayed(plan_a, 0, relay_a, keep_a)
    near_out(plan_b)
    relayed(plan_d, 1, relay_d, None)
    relayed(plan_b, 2, relay_b, None)

    def scatter_rest(i, firsts_a, firsts_b, sa, sb, fa, fb, done):
        two = [
            (ny, y, at_y, lambda to: sa.at[to], lambda k, o: fa.at[k - 1], two_send.at[i, 0], two_recv.at[i, 0]),
            (nz, z, at_z, lambda to: sb.at[to], lambda k, o: fb.at[k - 1], two_send.at[i, 1], two_recv.at[i, 1])]
        for firsts, second in ((firsts_a, two[0]), (firsts_b, two[1])):
            for plan, own, total, got in firsts:
                if own is not None:
                    total[...] = own[...].astype(F32)
                for k in arriving(plan[0]):
                    landed(*plan, k).wait_recv()
                    total[...] += got[k - 1].astype(F32)
            exchange(*second)
        for route, (plan, total, fin, me) in enumerate(((two[0], sa, fa, y), (two[1], sb, fb, z))):
            value = total[me]
            for k in range(1, plan[0]):
                landed(*plan, k).wait_recv()
                value = value + fin[k - 1]
            done(route, value)
        return two

    raw_first = first_phase(1, [
        (True, lambda zz, yy: everyone.at[zz, yy, pl.ds(0, CUT)]),
        (False, lambda zz, yy: everyone.at[zz, yy, pl.ds(CUT, 96 - CUT)])])

    def raw_done(route, value):
        if route == 0:
            raw_u[:CUT] = value
            everyone[z, y, :CUT] = value.astype(BF16)
        else:
            raw_u[CUT:] = value[:64 - CUT]
            raw_d[...] = value[64 - CUT:]
            everyone[z, y, CUT:] = value.astype(BF16)
        start_first(raw_first[route:route + 1])

    raw_two = scatter_rest(
        0, [(plan_a, None, sum_a, got_a)],
        [(plan_d, part_d.at[:, y], sum_b.at[:, pl.ds(64 - CUT, 32)], got_d),
         (plan_b, part_b.at[:, y], sum_b.at[:, pl.ds(0, 64 - CUT)], got_b)],
        sum_a, sum_b, fin_a, fin_b, raw_done)

    def hops(route):
        n, me, place = ((nz, z, at_z), (ny, y, at_y))[route]

        def block(offset, half=None):
            b = (me + n + offset) % n
            if route == 0:
                part = slice(None) if half is None else pl.ds(half * halves_y, halves_y)
                return everyone.at[b, part, pl.ds(0, CUT)]
            part = slice(None) if half is None else pl.ds(half * halves_z, halves_z)
            return everyone.at[part, b, pl.ds(CUT, 96 - CUT)]

        def copy(i, ref, offset):
            return remote(ref, ref, hop_send.at[route, i], hop_recv.at[route, i],
                          place((me + n + offset) % n))

        sent = [copy(0, block(0), 2), copy(1, block(0), -2), copy(2, block(0), 1), copy(3, block(0), -1),
                copy(4, block(-2), 1), copy(5, block(2), -1), copy(6, block(-2, 0), 2), copy(7, block(2, 1), -2)]
        came = [copy(0, block(-2), 2), copy(1, block(2), -2), copy(2, block(-1), 1), copy(3, block(1), -1),
                copy(4, block(-3), 1), copy(5, block(3), -1), copy(6, block(-4, 0), 2), copy(7, block(4, 1), -2)]
        return sent, came

    raw_hops = [hops(0), hops(1)]
    for route in range(2):
        wait_first(raw_first[route:route + 1])
        for copy in raw_hops[route][0][:4]:
            copy.start()
    for side in range(2):
        for sent, came in raw_hops:
            came[side].wait_recv()
            sent[4 + side].start()
            sent[6 + side].start()
    for sent, came in raw_hops:
        for copy in came[2:]:
            copy.wait_recv()

    flat_u = everyone[:, :, :64].reshape(2 * ff, RANK)
    mixed_u = two_halves(jnp.dot(united[...], flat_u, preferred_element_type=F32))
    flat_d = everyone[:, :, 64:].reshape(ff, RANK)
    mixed_d = two_halves(jnp.dot(hidden[...], flat_d, preferred_element_type=F32))
    rplan_a = along_z(1, 0, rpart_a, rgot_a)
    rplan_b = along_y(1, 1, rpart_b, rgot_b)
    rounds = ny // 2
    per_round = nz // rounds

    def store_right(i, block):
        rpart_a[i] = block

    def right_round(q, carry):
        for extra in range(per_round):
            row_out(q * per_round + extra, rplan_a, 3, rrelay_a, rkeep_a, rsum_a, store_right,
                    lambda columns: tdot(acts[:, :, columns].reshape(nt * tokens, tile), mixed_u))

        pair = (y // 2 + q + rounds // 2) % rounds
        rows = jnp.concatenate(
            [cot[:, :, pl.ds(pl.multiple_of(i * tile + pair * 128, 128), 128)].reshape(
                nt * tokens, 128) for i in range(nz)], axis=1)
        rpart_b[:, pl.ds(2 * pair, 2)] = folded(
            tdot(rows, mixed_d)).reshape(nz, 2, 64, RANK).astype(BF16)
        for extra in range(2):
            k = (2 * pair + extra + ny - y) % ny

            @pl.when(k == ny // 2)
            def _():
                far_out(rplan_b, 4, rrelay_b)

            @pl.when(is_near(k, ny))
            def _():
                send_one(rplan_b, k)
        return carry

    lax.fori_loop(0, rounds, right_round, 0)
    relayed(rplan_a, 3, rrelay_a, rkeep_a)
    relayed(rplan_b, 4, rrelay_b, None)

    row = lax.broadcasted_iota(jnp.int32, (RANK, RANK), 0)
    col = lax.broadcasted_iota(jnp.int32, (RANK, RANK), 1)
    for i, flat in enumerate((flat_u, flat_d)):
        gram[i, :, :RANK] = tdot(flat, flat)
        gram[i, :, RANK:] = (row == col).astype(F32)
    lane = lax.broadcasted_iota(jnp.int32, (PANEL, RANK), 1)
    sub = lax.broadcasted_iota(jnp.int32, (PANEL, RANK), 0)
    sub_one = lax.broadcasted_iota(jnp.int32, (PANEL, 1), 0)

    def eliminate(b, carry):
        base = pl.multiple_of(b * PANEL, PANEL)
        rows = pl.ds(base, PANEL)
        panels = [gram[i, rows, :] for i in range(2)]
        for j in range(PANEL):
            for i in range(2):
                panel = panels[i]
                column = jnp.sum(
                    jnp.where(lane == base + j, panel[:, :RANK], 0.0), axis=1, keepdims=True)
                factor = jnp.where(sub_one > j, column / column[j:j + 1], 0.0)
                panels[i] = panel - factor * panel[j:j + 1]
        for i in range(2):
            panel = panels[i]
            gram[i, rows, :] = panel
            head = panel[:, :RANK]
            pivots = jnp.sum(jnp.where(lane == base + sub, head, 0.0), axis=1, keepdims=True)
            weights = jnp.where(lane >= base + PANEL, head / pivots, 0.0)
            gram[i] -= lax.dot_general(
                weights, panel, (((0,), (0,)), ((), ())),
                precision=lax.Precision.HIGHEST, preferred_element_type=F32)
        return carry

    lax.fori_loop(0, RANK // PANEL, eliminate, 0)
    inverse = []
    for i in range(2):
        pivots = jnp.sum(jnp.where(row == col, gram[i, :, :RANK], 0.0), axis=1, keepdims=True)
        inverse.append(gram[i, :, RANK:] * lax.rsqrt(pivots))

    def solved(values, i):
        return lax.dot_general(
            values, inverse[i], (((1,), (1,)), ((), ())),
            precision=lax.Precision.HIGHEST, preferred_element_type=F32)

    packed_out[:64] = solved(raw_u[...], 0)
    packed_out[64:96] = solved(raw_d[...], 1)

    for copy in tok_sends:
        copy.wait_send()
    drain_first(warm_first + raw_first + raw_two)
    drain_one(plan_a, 0, relay_a)
    drain_one(plan_d, 1, relay_d)
    drain_one(plan_b, 2, relay_b)
    ring_drain(warm_ring)
    for sent, came in raw_hops:
        for copy in sent:
            copy.wait_send()

    def right_done(route, value):
        packed_out[96 + 64 * route:160 + 64 * route] = solved(value, route) * (1.0 / (nz * ny))

    right_two = scatter_rest(
        1, [(rplan_a, None, rsum_a, rgot_a)], [(rplan_b, rpart_b.at[:, y], rsum_b, rgot_b)],
        rsum_a, rsum_b, rfin_a, rfin_b, right_done)
    drain_first(right_two)
    drain_one(rplan_a, 3, rrelay_a)
    drain_one(rplan_b, 4, rrelay_b)


def unpack(packed, left_u, left_d, right):
    left_u[...] = packed[:64]
    left_d[...] = packed[64:96]
    right[0] = packed[96:160]
    right[1] = packed[160:224]


def on_device(shape, activations, cotangent, gate_pre, up_value, hidden_grad, warm_factors):
    nz, ny, nt = shape
    tokens, width = activations.shape
    rows, ff = gate_pre.shape
    cut_b = 96 - CUT
    half = max(nz, ny) // 2
    packed = pl.pallas_call(
        functools.partial(kernel, nz, ny, nt),
        out_shape=jax.ShapeDtypeStruct((224, RANK), F32),
        in_specs=[pl.BlockSpec(memory_space=pl.ANY)] * 6,
        out_specs=pl.BlockSpec(memory_space=pltpu.VMEM),
        scratch_shapes=[
            pltpu.VMEM((nt, tokens, width), BF16),
            pltpu.VMEM((nt, tokens, width), BF16),
            pltpu.VMEM((rows, ff), BF16),
            pltpu.VMEM((rows, ff), BF16),
            pltpu.VMEM((rows, ff), BF16),
            pltpu.VMEM((2, 1, 64, RANK), F32),
            pltpu.VMEM((2, nz, ny, 64 + FINE, RANK), BF16),
            pltpu.VMEM((rows, 2 * ff), BF16),
            pltpu.VMEM((rows, ff), BF16),
            pltpu.VMEM((nz, ny, CUT, RANK), BF16),
            pltpu.VMEM((nz, ny, 64 - CUT, RANK), BF16),
            pltpu.VMEM((nz, ny, 32, RANK), BF16),
            pltpu.VMEM((nz - 1, ny, CUT, RANK), BF16),
            pltpu.VMEM((ny - 1, nz, 64 - CUT, RANK), BF16),
            pltpu.VMEM((ny - 1, nz, 32, RANK), BF16),
            pltpu.VMEM((ny, CUT, RANK), F32),
            pltpu.VMEM((nz, cut_b, RANK), F32),
            pltpu.VMEM((ny - 1, CUT, RANK), F32),
            pltpu.VMEM((nz - 1, cut_b, RANK), F32),
            pltpu.VMEM((64, RANK), F32),
            pltpu.VMEM((32, RANK), F32),
            pltpu.VMEM((nz, ny, 96, RANK), BF16),
            pltpu.VMEM((nz, ny, 64, RANK), BF16),
            pltpu.VMEM((nz, ny, 64, RANK), BF16),
            pltpu.VMEM((nz - 1, ny, 64, RANK), BF16),
            pltpu.VMEM((ny - 1, nz, 64, RANK), BF16),
            pltpu.VMEM((ny, 64, RANK), F32),
            pltpu.VMEM((nz, 64, RANK), F32),
            pltpu.VMEM((ny - 1, 64, RANK), F32),
            pltpu.VMEM((nz - 1, 64, RANK), F32),
            pltpu.VMEM((2, RANK, 2 * RANK), F32),
            pltpu.VMEM((2, ny // 2, CUT, RANK), BF16),
            pltpu.VMEM((2, nz // 2, 32, RANK), BF16),
            pltpu.VMEM((2, nz // 2, 64 - CUT, RANK), BF16),
            pltpu.VMEM((2, ny // 2, 64, RANK), BF16),
            pltpu.VMEM((2, nz // 2, 64, RANK), BF16),
            pltpu.VMEM((2, ny, CUT, RANK), F32),
            pltpu.VMEM((2, ny, 64, RANK), F32),
            pltpu.SemaphoreType.DMA((6,)),
            pltpu.SemaphoreType.DMA((14,)),
            pltpu.SemaphoreType.DMA((14,)),
            pltpu.SemaphoreType.DMA((2, 2, max(nz, ny) - 1)),
            pltpu.SemaphoreType.DMA((2, 2, max(nz, ny) - 1)),
            pltpu.SemaphoreType.DMA((2, 4, half, 2)),
            pltpu.SemaphoreType.DMA((2, 4, half, 2)),
            pltpu.SemaphoreType.DMA((2, 3, max(nz, ny) - 1)),
            pltpu.SemaphoreType.DMA((2, 3, max(nz, ny) - 1)),
            pltpu.SemaphoreType.DMA((2, 2, max(nz, ny) - 1)),
            pltpu.SemaphoreType.DMA((2, 2, max(nz, ny) - 1)),
            pltpu.SemaphoreType.DMA((5, 2)),
            pltpu.SemaphoreType.DMA((5, 2)),
            pltpu.SemaphoreType.DMA((2, 8)),
            pltpu.SemaphoreType.DMA((2, 8)),
        ],
        compiler_params=pltpu.CompilerParams(
            collective_id=0, has_side_effects=True, vmem_limit_bytes=56 * 1024 * 1024),
        name="powersgd_step",
    )(activations, cotangent, gate_pre, up_value, hidden_grad, warm_factors)
    left_united, left_down, right = pl.pallas_call(
        unpack,
        out_shape=(
            jax.ShapeDtypeStruct((64, RANK), F32),
            jax.ShapeDtypeStruct((32, RANK), F32),
            jax.ShapeDtypeStruct((2, 64, RANK), F32)),
        name="unpack",
    )(packed)
    return left_united[None], left_down[None], right[:, None]


def solution(mesh):
    dp, nt = mesh.shape["dp"], mesh.shape["tensor"]
    ny = 1 << (dp.bit_length() // 2)
    in_specs = (
        P(("dp", "tensor"), None),
        P(("dp", "tensor"), None),
        P("dp", "tensor"),
        P("dp", "tensor"),
        P("dp", "tensor"),
        P(None, "tensor", "dp", None),
    )
    out_specs = (P("tensor", "dp", None), P("tensor", "dp", None), P(None, "tensor", "dp", None))
    return jax.shard_map(
        functools.partial(on_device, (dp // ny, ny, nt)),
        mesh=mesh, in_specs=in_specs, out_specs=out_specs, check_vma=False)
```
